512 devices in a mesh: dp: 32 (over y, x), ctx: 16 (over z, core).
Axes of the slice: x: 4, y: 8, z: 8, core: 2. Of those that a mesh axis runs over, the one named last changes fastest.
Arguments:
- queries: bfloat16 [32, 2048, 1024], P('dp', 'ctx'), may hold values from -6 to 6
- key_rows: bfloat16 [32, 2048, 128], P('dp', 'ctx'), may hold values from -6 to 6
- x_rows: bfloat16 [32, 2048, 4096], P('dp', 'ctx'), may hold values from -6 to 6
- value_weight: bfloat16 [4096, 128], replicated, may hold values from -0.09375 to 0.09375
- grad_context: bfloat16 [32, 2048, 1024], P('dp', 'ctx'), may hold values from -6 to 6
- doc_lengths: int32 [32, 8], P('dp'), may hold values from 1 to 1024, 2048 in all within a row
- block_order: int32 [32, 16], P('dp'), may hold values from 0 to 15, each once within a row
Outputs:
- context: bfloat16 [32, 2048, 1024], P('dp', 'ctx')
- grad_queries: bfloat16 [32, 2048, 1024], P('dp', 'ctx')
- grad_keys: bfloat16 [32, 2048, 128], P('dp', 'ctx')
- grad_values: bfloat16 [32, 2048, 128], P('dp', 'ctx')
- grad_weight: float32 [4096, 128], P(('dp', 'ctx'))
The draws below stay inside these ranges and needn't reach their ends.
Inputs may be any that keep to these rules, and one draw needn't show every extreme that they name: `doc_lengths`: each row is the document lengths of one microbatch in order, summing to 2048; the longest is exactly 1024. `block_order`: each row is a permutation of the 16 sequence blocks.
All inputs are finite; a program needn't handle non-finite values.
Results may differ from the reference program's by a relative error of at most 0.019.
Values may be sent and summed in bfloat16 or wider, within the bound.
A program may use at most 64 MiB of HBM per device.

```python
import math
import jax
import jax.numpy as jnp
import numpy as np
from jax import lax

HQ = 8
HD = 128
D = 4096
BLOCK = 128
DOCS = 8
MICRO = 32
SEQ = 2048
NBLK = 16
N_CTX = 16


def draw_queries(key, part):
    key = jax.random.fold_in(key, 11)
    first_key = jax.random.fold_in(key, 0)
    full_shape = (MICRO, SEQ, HQ, HD)
    sample = jnp.clip(jax.random.normal(first_key, full_shape), -4.0, 4.0)
    return sample.reshape(MICRO, SEQ, HQ * HD).astype(jnp.bfloat16)


def draw_key_rows(key, part):
    key = jax.random.fold_in(key, 23)
    first_key = jax.random.fold_in(key, 0)
    full_shape = (MICRO, SEQ, HD)
    sample = jnp.clip(jax.random.normal(first_key, full_shape), -4.0, 4.0)
    return sample.astype(jnp.bfloat16)


def spiked(result, rng, source, target, shards_of, factor):
    def block_of(position):
        return (jnp.arange(result.shape[position]) // (result.shape[position] // shards_of)).reshape((-1,) + (1,) * (result.ndim - 1 - position))

    near = jax.random.permutation(rng, shards_of)[block_of(target)]
    second = (block_of(target) + shards_of // 2) % shards_of
    return jnp.where((block_of(source) == near) | (block_of(source) == second), factor * result, result)


def steps_of(key, dims, cuts, least, top_value):
    def one(dim, shards_of):
        heights = jax.random.uniform(jax.random.fold_in(jax.random.fold_in(key, 6), dim), (shards_of,), jnp.float32, least / len(cuts), top_value / len(cuts))
        return jnp.repeat(jnp.exp(heights), dims[dim] // shards_of).reshape((-1,) + (1,) * (len(dims) - dim - 1))

    factor_of = one(*cuts[0])
    for cut in cuts[1:]:
        factor_of = factor_of * one(*cut)
    return factor_of


def length_profile(count, total, bound, skew):
    loads = [(1 << 20) // math.isqrt(standing ** skew) + 1 for standing in range(2, count + 1)]
    rest, holding = total - bound - (count - 1), [1] * (count - 1)
    while rest > 0:
        free = [i for i in range(count - 1) if holding[i] < bound]
        pool, budget = sum([loads[i] for i in free]), rest
        for i in free:
            addition = min(bound - holding[i], max(1, budget * loads[i] // pool), rest)
            holding[i] = holding[i] + addition
            rest = rest - addition
    return np.array([bound] + holding)


def uneven(key, amount, total, limit, skew):
    if amount == 2:
        one = jax.random.randint(key, (), max(1, total - limit), min(limit, total - 1) + 1)
        return jnp.stack([one, total - one])
    sizes = jnp.asarray(length_profile(amount, total, limit, skew), jnp.int32)
    couples = (amount - 1) // 2
    giver, receiver = sizes[1:1 + 2 * couples:2], sizes[2:2 + 2 * couples:2]
    slack = jnp.minimum(giver - 1, limit - receiver)
    passed = jax.random.randint(jax.random.fold_in(key, 1), (couples,), 0, 1 << 20) % (slack + 1)
    sizes = sizes.at[1:1 + 2 * couples:2].set(giver - passed).at[2:2 + 2 * couples:2].set(receiver + passed)
    return sizes[jax.random.permutation(jax.random.fold_in(key, 2), amount)]


def centred(stream_key, shape, scale, most, cuts=(), held_as=jnp.bfloat16):
    array = scale * jax.random.normal(stream_key, shape, jnp.float32)
    if cuts:
        array = array * steps_of(stream_key, shape, cuts, -0.22, 0.18)
    return jnp.clip(array, -most, most).astype(held_as)


def heavy_noise(own_key, extent, scale, limit, cuts, heavy, held_as=jnp.bfloat16):
    array = scale * jax.random.normal(own_key, extent, jnp.float32)
    if cuts:
        array = array * steps_of(own_key, extent, cuts, -0.22, 0.18)
    return jnp.clip(spiked(array, jax.random.fold_in(own_key, 3), *heavy), -limit, limit).astype(held_as)


def setup_inputs(seed: int = 0) -> dict:
    splits = jax.random.split(jax.random.key(seed), 8)
    queries = draw_queries(jax.random.fold_in(splits[7], 71), 0)
    key_rows = draw_key_rows(jax.random.fold_in(splits[7], 71), 0)
    x_rows = heavy_noise(splits[2], (MICRO, SEQ, D), 1.0, 6.0, ((0, 32), (1, 16)), (1, 2, 16, 2.0))
    value_weight = centred(splits[3], (D, HD), D ** -0.5, 0.09375)
    grad_context = centred(splits[4], (MICRO, SEQ, HQ * HD), 1.0, 6.0, ((0, 32), (1, 16)))
    doc_lengths = jax.vmap(lambda own: uneven(own, DOCS, SEQ, SEQ // 2, 2))(jax.random.split(splits[5], MICRO)).reshape((MICRO, DOCS)).astype(jnp.int32)
    block_order = jax.vmap(lambda own: jax.random.permutation(own, NBLK))(jax.random.split(splits[6], MICRO)).reshape((MICRO, NBLK)).astype(jnp.int32)
    return {"queries": queries, "key_rows": key_rows, "x_rows": x_rows, "value_weight": value_weight, "grad_context": grad_context, "doc_lengths": doc_lengths, "block_order": block_order}


def doc_ids(lengths, positions):
    ends = jnp.cumsum(lengths).astype(jnp.int32)
    return lax.optimization_barrier(jnp.sum((positions[:, None] >= ends[None, :]).astype(jnp.int32), axis=1))

def reference(queries, key_rows, x_rows, value_weight, grad_context, doc_lengths, block_order):
    score_scale = 1.0 / math.sqrt(HD)
    per_device = SEQ // N_CTX

    def one_micro(pieces):
        query_block, key_block, input_block, grad_block, lengths, order_row = pieces
        value_rows = jnp.dot(input_block, value_weight, preferred_element_type=jnp.float32).astype(jnp.bfloat16)
        offsets = jnp.arange(BLOCK, dtype=jnp.int32)
        query_pos = (order_row.astype(jnp.int32)[:, None] * BLOCK + offsets[None, :]).reshape(SEQ)
        key_pos = jnp.arange(SEQ, dtype=jnp.int32)
        allowed = (doc_ids(lengths, query_pos)[:, None] == doc_ids(lengths, key_pos)[None, :]) & (key_pos[None, :] <= query_pos[:, None])
        query_heads = query_block.reshape(SEQ, HQ, HD).transpose(1, 0, 2)
        grad_heads = grad_block.reshape(SEQ, HQ, HD).transpose(1, 0, 2)

        def head_step(running, head_pieces):
            query_head, grad_head = head_pieces
            scores = jnp.dot(query_head, key_block.T, preferred_element_type=jnp.float32) * score_scale
            scores = jnp.where(allowed, scores, -jnp.inf)
            row_max = lax.optimization_barrier(jnp.max(scores, axis=1, keepdims=True))
            exp_scores = jnp.exp(scores - row_max)
            prob = exp_scores / lax.optimization_barrier(jnp.sum(exp_scores, axis=1, keepdims=True))
            weights = prob.astype(jnp.bfloat16)
            context = jnp.dot(weights, value_rows, preferred_element_type=jnp.float32).astype(jnp.bfloat16)
            delta = lax.optimization_barrier(jnp.sum(grad_head.astype(jnp.float32) * context.astype(jnp.float32), axis=1, keepdims=True))
            grad_prob = jnp.dot(grad_head, value_rows.T, preferred_element_type=jnp.float32)
            grad_scores = (prob * (grad_prob - delta) * score_scale).astype(jnp.bfloat16)
            grad_query = jnp.dot(grad_scores, key_block, preferred_element_type=jnp.float32).astype(jnp.bfloat16)
            key_part = jnp.einsum('crs,crd->csd', grad_scores.reshape(N_CTX, per_device, SEQ).astype(jnp.float32), query_head.reshape(N_CTX, per_device, HD).astype(jnp.float32), precision=lax.Precision.HIGHEST)
            value_part = jnp.einsum('crs,crd->csd', weights.reshape(N_CTX, per_device, SEQ).astype(jnp.float32), grad_head.reshape(N_CTX, per_device, HD).astype(jnp.float32), precision=lax.Precision.HIGHEST)
            return ((running[0] + key_part, running[1] + value_part), (context, grad_query))
        start = (jnp.zeros((N_CTX, SEQ, HD), jnp.float32), jnp.zeros((N_CTX, SEQ, HD), jnp.float32))
        (key_parts, value_parts), (context_heads, grad_query_heads) = lax.scan(head_step, start, (query_heads, grad_heads))

        def settle(parts):
            rounded = lax.optimization_barrier(parts.astype(jnp.bfloat16))
            return lax.optimization_barrier(jnp.sum(rounded.astype(jnp.float32), axis=0)).astype(jnp.bfloat16)
        grad_keys = settle(key_parts)
        grad_values = settle(value_parts)
        context = context_heads.transpose(1, 0, 2).reshape(SEQ, HQ * HD)
        grad_queries = grad_query_heads.transpose(1, 0, 2).reshape(SEQ, HQ * HD)
        weight_term = jnp.dot(input_block.T, grad_values, preferred_element_type=jnp.float32)
        return (context, grad_queries, grad_keys, grad_values, weight_term)
    results = lax.map(one_micro, (queries, key_rows, x_rows, grad_context, doc_lengths, block_order))
    grad_weight = lax.optimization_barrier(jnp.sum(results[4], axis=0))
    return (results[0], results[1], results[2], results[3], grad_weight)
```

```python
import functools
import math

import jax
import jax.numpy as jnp
from jax import lax
from jax.experimental import pallas as pl
from jax.experimental.pallas import tpu as pltpu
from jax.sharding import PartitionSpec as P

BLOCK = 128
MESH = pl.DeviceIdType.MESH
NEG = -1e30


def remote(src, dst, send_sem, recv_sem, device):
    return pltpu.make_async_remote_copy(
        src_ref=src,
        dst_ref=dst,
        send_sem=send_sem,
        recv_sem=recv_sem,
        device_id=device,
        device_id_type=MESH,
    )


def dot(a, b):
    return jnp.dot(a, b, preferred_element_type=jnp.float32)


def kernel(
    nx, ny, nz, heads,
    q_hbm, k_hbm, x_hbm, w_hbm, gc_hbm, len_s, ord_s,
    ctx_o, gq_o, gk_o, gv_o, gw_o,
    q_v, gc_v, x_v, w_v, kv, qn, qt, gcn, gct, bias, kw, vw, kwt, vwt,
    kacc, vacc, pad, sib_out, sib_in, rs_out, rs_in, ctx_v, gq_v, gkv_v,
    xg, xgt, gvg, p_out, p_in, r_v, r_in, gw_v,
    load_sem, store_sem, ring_send, ring_recv, sib_send, sib_recv,
    half_send, half_recv, rs_send, rs_recv, xg_send, xg_recv,
    gv_send, gv_recv, p_send, p_recv, r_send, r_recv,
):
    nc = 2 * nz
    wb = nc // 2 + 1
    pb = nc - wb
    yc = ny // 2
    ng = 2 * nx
    fr = BLOCK // nc
    pairs = heads // 2
    span = wb * BLOCK
    d = lax.axis_index("dp")
    c = lax.axis_index("ctx")
    y = lax.div(d, nx)
    x = lax.rem(d, nx)
    z = lax.div(c, 2)
    k = lax.rem(c, 2)
    g = 2 * x + k
    score_scale = 1.0 / math.sqrt(BLOCK)

    def at_z(other):
        return {"ctx": 2 * lax.rem(other, nz) + k}

    sibling = {"ctx": 2 * z + 1 - k}

    def load(src, dst, n):
        return pltpu.make_async_copy(src, dst, load_sem.at[n])

    load_k = load(k_hbm, kv.at[0, c], 0)
    load_x = load(x_hbm, x_v, 1)
    load_w = load(w_hbm, w_v, 2)
    load_q = load(q_hbm, q_v, 3)
    load_gc = load(gc_hbm, gc_v, 4)
    for one in (load_k, load_x, load_w, load_q, load_gc):
        one.start()

    barrier = pltpu.get_barrier_semaphore()
    count = 0
    for s in range(1, nc):
        pl.semaphore_signal(barrier, 1, device_id={"ctx": lax.rem(c + s, nc)}, device_id_type=MESH)
        count += 1
    for s in range(1, nx):
        for kk in range(2):
            pl.semaphore_signal(
                barrier, 1,
                device_id={"dp": y * nx + lax.rem(x + s, nx), "ctx": 2 * z + kk},
                device_id_type=MESH,
            )
            count += 1
    for s in range(1, ny):
        pl.semaphore_signal(
            barrier, 1, device_id={"dp": lax.rem(y + s, ny) * nx + x}, device_id_type=MESH
        )
        count += 1
    pl.semaphore_wait(barrier, count)

    reach = ((nz // 2, nz - 1 - nz // 2), (nz - 1 - nz // 2, nz // 2))

    def ring(t, zs, way):
        slot = kv.at[t, 2 * zs + k]
        step = 1 if way == 0 else nz - 1
        return remote(slot, slot, ring_send.at[t, way, zs], ring_recv.at[t, zs], at_z(z + step))

    def to_sibling(t, zs):
        slot = kv.at[t, 2 * zs + k]
        return remote(slot, slot, sib_send.at[t, zs], sib_recv.at[t, zs], sibling)

    def origin(way, s):
        return lax.rem(z + nz - s, nz) if way == 0 else lax.rem(z + s, nz)

    def ring_begin(t):
        for way in range(2):
            if reach[t][way] > 0:
                ring(t, z, way).start()
        to_sibling(t, z).start()

    def ring_step(t, s):
        for way in range(2):
            if s <= reach[t][way]:
                zs = origin(way, s)
                ring(t, zs, way).wait_recv()
                if s < reach[t][way]:
                    ring(t, zs, way).start()
                to_sibling(t, zs).start()

    load_k.wait()
    ring_begin(0)

    def x_columns(kk, xx, i):
        return pl.ds(pl.multiple_of(((kk * yc + i) * nx + xx) * BLOCK, BLOCK), BLOCK)

    def group(s):
        gg = lax.rem(g + s, ng)
        xx = lax.div(gg, 2)
        kk = lax.rem(gg, 2)
        return gg, xx, kk, {"dp": y * nx + xx, "ctx": 2 * z + kk}

    for s in range(1, ng):
        gg, xx, kk, device = group(s)
        for i in range(yc):
            remote(
                x_hbm.at[:, x_columns(kk, xx, i)], xg.at[g, i], xg_send.at[gg], xg_recv.at[g], device
            ).start()

    load_x.wait()
    load_w.wait()
    kv[1, c] = dot(x_v[...], w_v[...]).astype(jnp.bfloat16)
    ring_begin(1)

    ring_step(0, 1)

    load_q.wait()
    load_gc.wait()

    def split_heads(src, upright, turned):
        for h in range(heads):
            part = src[:, h * BLOCK : (h + 1) * BLOCK]
            rows = slice((h % 2) * BLOCK, (h % 2 + 1) * BLOCK)
            upright[h // 2, rows, :] = part
            turned[h // 2, :, rows] = part.T

    split_heads(q_v, qn, qt)
    ring_step(1, 1)
    if nz > 2:
        ring_step(0, 2)
    split_heads(gc_v, gcn, gct)
    if nz > 2:
        ring_step(1, 2)

    block = ord_s[0, c]
    first = jnp.maximum(block - (wb - 1), 0)
    query_pos = block * BLOCK + lax.broadcasted_iota(jnp.int32, (1, BLOCK), 1)
    low = jnp.zeros((1, BLOCK), jnp.int32)
    end = jnp.int32(0)
    for i in range(len_s.shape[1]):
        end = end + len_s[0, i]
        low = jnp.where(query_pos >= end, end, low)
    key_pos = first * BLOCK + lax.broadcasted_iota(jnp.int32, (span, BLOCK), 0)
    bias[...] = jnp.where((key_pos >= low) & (key_pos <= query_pos), 0.0, NEG)
    kacc[...] = jnp.zeros_like(kacc)
    vacc[...] = jnp.zeros_like(vacc)
    for t in range(2):
        for i in range(pb + nc):
            if i < pb or i >= pb + wb:
                pad[t, i] = jnp.zeros((BLOCK, BLOCK), jnp.bfloat16)

    for s in range(3, nz // 2 + 1):
        ring_step(0, s)
        ring_step(1, s)
    for t in range(2):
        for zs in range(nz):
            slot = kv.at[t, 2 * zs + 1 - k]
            remote(slot, slot, sib_send.at[t, zs], sib_recv.at[t, zs], sibling).wait_recv()

    for i in range(wb):
        rows = slice(i * BLOCK, (i + 1) * BLOCK)
        key_block = kv[0, first + i]
        value_block = kv[1, first + i]
        kw[rows, :] = key_block
        vw[rows, :] = value_block
        kwt[:, rows] = key_block.T
        vwt[:, rows] = value_block.T
    log_scale = score_scale * math.log2(math.e)

    def attend(p, carry):
        scores = dot(kw[...], qt[p]) + jnp.concatenate([bias[...], bias[...]], axis=1)
        row_max = jnp.max(scores, axis=0, keepdims=True)
        exp_scores = jnp.exp2(scores * log_scale - row_max * log_scale)
        prob = exp_scores * (1.0 / jnp.sum(exp_scores, axis=0, keepdims=True))
        weights = prob.astype(jnp.bfloat16)
        context = dot(vwt[...], weights).astype(jnp.bfloat16)
        turned = gct[p]
        delta = jnp.sum(
            turned.astype(jnp.float32) * context.astype(jnp.float32), axis=0, keepdims=True
        )
        grad_prob = dot(vw[...], turned)
        grad_scores = (prob * (grad_prob - delta)).astype(jnp.bfloat16)
        grad_query = (dot(kwt[...], grad_scores) * score_scale).astype(jnp.bfloat16)
        vacc[...] += dot(weights, gcn[p])
        kacc[...] += dot(grad_scores, qn[p])
        for i in range(2):
            columns = pl.ds(pl.multiple_of((2 * p + i) * BLOCK, BLOCK), BLOCK)
            lanes = slice(i * BLOCK, (i + 1) * BLOCK)
            ctx_v[:, columns] = context[:, lanes].T
            gq_v[:, columns] = grad_query[:, lanes].T
        return carry

    lax.fori_loop(0, pairs, attend, 0)
    store_ctx = pltpu.make_async_copy(ctx_v, ctx_o, store_sem.at[0])
    store_gq = pltpu.make_async_copy(gq_v, gq_o, store_sem.at[1])

    def half(t):
        return remote(sib_out.at[t], sib_in.at[t], half_send.at[t], half_recv.at[t], sibling)

    for t, acc, factor in ((1, vacc, 1.0), (0, kacc, score_scale)):
        for i in range(wb):
            pad[t, pb + i] = (acc[i * BLOCK : (i + 1) * BLOCK, :] * factor).astype(jnp.bfloat16)
        for zs in range(nz):
            sib_out[t, zs] = pad[t, pb + 2 * zs + 1 - k - first]
        half(t).start()
    store_ctx.start()
    store_gq.start()

    def scatter(t, s):
        zs = lax.rem(z + s, nz)
        return remote(
            rs_out.at[t, zs], rs_in.at[t, z], rs_send.at[t, zs], rs_recv.at[t, z], at_z(z + s)
        )

    def pair_sums(t):
        half(t).wait_recv()
        for zs in range(nz):
            both = pad[t, pb + 2 * zs + k - first].astype(jnp.float32) + sib_in[t, zs].astype(
                jnp.float32
            )
            rs_out[t, zs] = both.astype(jnp.bfloat16)

    def gathered(t):
        total = rs_out[t, z].astype(jnp.float32)
        for s in range(1, nz):
            zs = lax.rem(z + s, nz)
            remote(
                rs_out.at[t, zs], rs_in.at[t, zs], rs_send.at[t, zs], rs_recv.at[t, zs], at_z(z + s)
            ).wait_recv()
            total += rs_in[t, zs].astype(jnp.float32)
        return total.astype(jnp.bfloat16)

    pair_sums(1)
    for s in range(1, nz):
        scatter(1, s).start()
    pair_sums(0)

    for s in range(1, ng):
        gg, xx, kk, device = group(s)
        remote(xg.at[gg], xg.at[gg], xg_send.at[gg], xg_recv.at[gg], device).wait_recv()
    for i in range(yc):
        xg[g, i] = x_v[:, x_columns(k, x, i)]
    for gg in range(ng):
        for i in range(yc):
            xgt[i, :, gg * BLOCK : (gg + 1) * BLOCK] = xg[gg, i].T

    grad_values = gathered(1)
    gvg[g] = grad_values

    def share(s):
        gg, xx, kk, device = group(s)
        return remote(gvg.at[g], gvg.at[g], gv_send.at[gg], gv_recv.at[g], device)

    for s in range(1, ng):
        share(s).start()
    for s in range(1, nz):
        scatter(0, s).start()
    store_gv = pltpu.make_async_copy(gvg.at[g], gv_o, store_sem.at[2])
    store_gv.start()
    for s in range(1, ng):
        gg, xx, kk, device = group(s)
        remote(gvg.at[gg], gvg.at[gg], gv_send.at[gg], gv_recv.at[gg], device).wait_recv()

    group_rows = gvg[...].reshape(ng * BLOCK, BLOCK)

    def to_y(i):
        yy = k * yc + i
        return yy, remote(
            p_out.at[i], p_in.at[y], p_send.at[i], p_recv.at[y], {"dp": yy * nx + x}
        )

    for i in range(yc):
        p_out[i] = dot(xgt[i], group_rows).astype(jnp.bfloat16)
        yy, copy = to_y(i)
        pl.when(yy != y)(copy.start)

    collects = lax.div(y, yc) == k

    def to_ctx(s):
        other = lax.rem(c + s, nc)
        rows = pl.ds(pl.multiple_of(other * fr, fr), fr)
        return remote(r_v.at[rows], r_in.at[z], r_send.at[s], r_recv.at[z], {"ctx": other})

    @pl.when(collects)
    def _():
        total = p_out[lax.rem(y, yc)].astype(jnp.float32)
        for s in range(1, ny):
            yy = lax.rem(y + s, ny)
            remote(
                p_in.at[yy], p_in.at[yy], p_send.at[0], p_recv.at[yy], {"dp": yy * nx + x}
            ).wait_recv()
            total += p_in[yy].astype(jnp.float32)
        r_v[...] = total
        for s in range(1, nc):
            to_ctx(s).start()
        r_in[z] = r_v[pl.ds(pl.multiple_of(c * fr, fr), fr), :]

    gkv_v[...] = gathered(0)
    store_gk = pltpu.make_async_copy(gkv_v, gk_o, store_sem.at[3])
    store_gk.start()

    for zs in range(nz):
        @pl.when(jnp.logical_not(collects & (z == zs)))
        def _():
            remote(
                r_in.at[zs], r_in.at[zs], r_send.at[0], r_recv.at[zs], sibling
            ).wait_recv()

    gw_v[...] = jnp.sum(r_in[...], axis=0)
    store_gw = pltpu.make_async_copy(gw_v, gw_o, store_sem.at[4])
    store_gw.start()

    for t in range(2):
        for way in range(2):
            for s in range(reach[t][way]):
                ring(t, origin(way, s), way).wait_send()
        for zs in range(nz):
            to_sibling(t, zs).wait_send()
        half(t).wait_send()
        for s in range(1, nz):
            scatter(t, s).wait_send()
    for s in range(1, ng):
        gg, xx, kk, device = group(s)
        remote(xg.at[gg], xg.at[gg], xg_send.at[gg], xg_recv.at[gg], device).wait_send()
        share(s).wait_send()
    for i in range(yc):
        yy, copy = to_y(i)
        pl.when(yy != y)(copy.wait_send)

    @pl.when(collects)
    def _():
        for s in range(1, nc):
            to_ctx(s).wait_send()

    for one in (store_ctx, store_gq, store_gv, store_gk, store_gw):
        one.wait()


def body(nx, ny, nz, queries, key_rows, x_rows, value_weight, grad_context, doc_lengths, block_order):
    rows, width = queries.shape[1:]
    features = x_rows.shape[2]
    heads = width // BLOCK
    nc = 2 * nz
    wb = nc // 2 + 1
    pb = nc - wb
    yc = ny // 2
    ng = 2 * nx
    fr = BLOCK // nc
    pairs = heads // 2
    span = wb * BLOCK
    bf16, f32 = jnp.bfloat16, jnp.float32
    sq = (BLOCK, BLOCK)
    anywhere = pl.BlockSpec(memory_space=pl.ANY)
    scalars = pl.BlockSpec(memory_space=pltpu.SMEM)
    dma = pltpu.SemaphoreType.DMA
    outs = pl.pallas_call(
        functools.partial(kernel, nx, ny, nz, heads),
        out_shape=(
            jax.ShapeDtypeStruct((rows, width), bf16),
            jax.ShapeDtypeStruct((rows, width), bf16),
            jax.ShapeDtypeStruct(sq, bf16),
            jax.ShapeDtypeStruct(sq, bf16),
            jax.ShapeDtypeStruct((fr, BLOCK), f32),
        ),
        in_specs=[anywhere] * 5 + [scalars] * 2,
        out_specs=(anywhere,) * 5,
        scratch_shapes=[
            pltpu.VMEM((rows, width), bf16),
            pltpu.VMEM((rows, width), bf16),
            pltpu.VMEM((rows, features), bf16),
            pltpu.VMEM((features, BLOCK), bf16),
            pltpu.VMEM((2, nc) + sq, bf16),
            pltpu.VMEM((pairs, 2 * BLOCK, BLOCK), bf16),
            pltpu.VMEM((pairs, BLOCK, 2 * BLOCK), bf16),
            pltpu.VMEM((pairs, 2 * BLOCK, BLOCK), bf16),
            pltpu.VMEM((pairs, BLOCK, 2 * BLOCK), bf16),
            pltpu.VMEM((span, BLOCK), f32),
            pltpu.VMEM((span, BLOCK), bf16),
            pltpu.VMEM((span, BLOCK), bf16),
            pltpu.VMEM((BLOCK, span), bf16),
            pltpu.VMEM((BLOCK, span), bf16),
            pltpu.VMEM((span, BLOCK), f32),
            pltpu.VMEM((span, BLOCK), f32),
            pltpu.VMEM((2, pb + nc) + sq, bf16),
            pltpu.VMEM((2, nz) + sq, bf16),
            pltpu.VMEM((2, nz) + sq, bf16),
            pltpu.VMEM((2, nz) + sq, bf16),
            pltpu.VMEM((2, nz) + sq, bf16),
            pltpu.VMEM((rows, width), bf16),
            pltpu.VMEM((rows, width), bf16),
            pltpu.VMEM(sq, bf16),
            pltpu.VMEM((ng, yc) + sq, bf16),
            pltpu.VMEM((yc, BLOCK, ng * BLOCK), bf16),
            pltpu.VMEM((ng,) + sq, bf16),
            pltpu.VMEM((yc,) + sq, bf16),
            pltpu.VMEM((ny,) + sq, bf16),
            pltpu.VMEM(sq, f32),
            pltpu.VMEM((nz, fr, BLOCK), f32),
            pltpu.VMEM((fr, BLOCK), f32),
            dma((5,)),
            dma((5,)),
            dma((2, 2, nz)),
            dma((2, nz)),
            dma((2, nz)),
            dma((2, nz)),
            dma((2,)),
            dma((2,)),
            dma((2, nz)),
            dma((2, nz)),
            dma((ng,)),
            dma((ng,)),
            dma((ng,)),
            dma((ng,)),
            dma((yc,)),
            dma((ny,)),
            dma((nc,)),
            dma((nz,)),
        ],
        compiler_params=pltpu.CompilerParams(
            collective_id=0, has_side_effects=True, vmem_limit_bytes=40 * 1024 * 1024
        ),
        name="attention_core",
    )(
        queries[0], key_rows[0], x_rows[0], value_weight, grad_context[0], doc_lengths, block_order
    )
    context, grad_queries, grad_keys, grad_values, grad_weight = outs
    return (context[None], grad_queries[None], grad_keys[None], grad_values[None], grad_weight)


def solution(mesh, sizes=(4, 8, 8)):
    placed = (
        P("dp", "ctx", None),
        P("dp", "ctx", None),
        P("dp", "ctx", None),
        P(),
        P("dp", "ctx", None),
        P("dp", None),
        P("dp", None),
    )
    return jax.shard_map(
        functools.partial(body, *sizes),
        mesh=mesh,
        in_specs=placed,
        out_specs=(
            P("dp", "ctx", None),
            P("dp", "ctx", None),
            P("dp", "ctx", None),
            P("dp", "ctx", None),
            P(("dp", "ctx"), None),
        ),
        check_vma=False,
    )
```

```python
import functools
import math

import jax
import jax.numpy as jnp
from jax import lax
from jax.experimental import pallas as pl
from jax.experimental.pallas import tpu as pltpu
from jax.sharding import PartitionSpec as P

BLOCK = 128
MESH = pl.DeviceIdType.MESH
NEG = -1e30
VMEM_LIMIT = 60 * 1024 * 1024


def remote(src, dst, send_sem, recv_sem, device):
    return pltpu.make_async_remote_copy(
        src_ref=src,
        dst_ref=dst,
        send_sem=send_sem,
        recv_sem=recv_sem,
        device_id=device,
        device_id_type=MESH,
    )


def dot(a, b):
    return jnp.dot(a, b, preferred_element_type=jnp.float32)


def kernel(
    nx, ny, nz, heads,
    q_hbm, k_hbm, x_hbm, w_hbm, gc_hbm, len_s, ord_s,
    ctx_o, gq_o, gk_o, gv_o, gw_o,
    q_v, gc_v, x_v, w_v, k_all, v_all, qn, qt, gcn, gct, bias, kw, vw, kwt, vwt,
    wt, kacc, vacc, pad, sib_out, sib_in, rs_out, rs_in, ctx_v, gq_v, gkv_v,
    x_out, xg, xgt, gvg, p_out, p_in, r_v, r_in, gw_v,
    load_sem, store_sem, hop_send, hop_recv, far_send, far_recv, sib_send, sib_recv,
    half_send, half_recv, rs_send, rs_recv, xg_send, xg_recv,
    gv_send, gv_recv, p_send, p_recv, r_send, r_recv,
):
    nc = 2 * nz
    wb = nc // 2 + 1
    pb = nc - wb
    yc = ny // 2
    ng = 2 * nx
    fr = BLOCK // nc
    pairs = heads // 2
    span = wb * BLOCK
    d = lax.axis_index("dp")
    c = lax.axis_index("ctx")
    y = lax.div(d, nx)
    x = lax.rem(d, nx)
    z = lax.div(c, 2)
    k = lax.rem(c, 2)
    g = 2 * x + k
    kv = (k_all, v_all)
    score_scale = 1.0 / math.sqrt(BLOCK)

    sibling = {"ctx": 2 * z + 1 - k}

    def load(src, dst, n):
        return pltpu.make_async_copy(src, dst, load_sem.at[n])

    load_k = load(k_hbm, k_all.at[c], 0)
    load_x = load(x_hbm, x_v, 1)
    load_w = load(w_hbm, w_v, 2)
    load_q = load(q_hbm, q_v, 3)
    load_gc = load(gc_hbm, gc_v, 4)
    for one in (load_k, load_x, load_w, load_q, load_gc):
        one.start()

    barrier = pltpu.get_barrier_semaphore()
    partners = [{"ctx": 2 * lax.rem(z + s, nz) + k} for s in range(1, nz)] + [sibling]
    for kk in range(2):
        for s in range(1, nx):
            partners.append({"dp": y * nx + lax.rem(x + s, nx), "ctx": 2 * z + kk})
        for s in range(1, ny):
            partners.append({"dp": lax.rem(y + s, ny) * nx + x, "ctx": 2 * z + kk})
    for device in partners:
        pl.semaphore_signal(barrier, 1, device_id=device, device_id_type=MESH)
    pl.semaphore_wait(barrier, len(partners))

    low_half, high_half = pl.ds(0, BLOCK // 2), pl.ds(BLOCK // 2, BLOCK // 2)

    def at(s):
        return lax.rem(z + (s + 2 * nz), nz)

    def hop(t, zs, s, part=None):
        slot = kv[t].at[2 * zs + k]
        if part is None:
            return remote(
                slot, slot, hop_send.at[t, zs, s + 2], hop_recv.at[t, zs], {"ctx": 2 * at(s) + k}
            )
        slot = slot.at[high_half if part else low_half]
        return remote(
            slot, slot, far_send.at[t, part], far_recv.at[t, part], {"ctx": 2 * at(s) + k}
        )

    def to_sibling(t, zs):
        slot = kv[t].at[2 * zs + k]
        return remote(slot, slot, sib_send.at[t, zs], sib_recv.at[t, zs], sibling)

    near = (2, -2, 1, -1) if nz == 8 else ((1, -1, 2) if nz == 4 else (1,))
    relays = ((-2, 1), (2, -1)) if nz == 8 else ()

    def direct(t):
        for s in near:
            hop(t, z, s).start()
        to_sibling(t, z).start()

    def relay(t):
        for source, s in relays:
            zs = at(source)
            hop(t, zs, s).wait_recv()
            hop(t, zs, 2 * s, 0 if s > 0 else 1).start()
            hop(t, zs, s).start()
            to_sibling(t, zs).start()
        for s in near:
            if s not in (2, -2) or nz != 8:
                hop(t, at(-s), s).wait_recv()
                to_sibling(t, at(-s)).start()

    def settle(t):
        if nz == 8:
            for s in (1, -1):
                zs = at(-3 * s)
                hop(t, zs, s).wait_recv()
                to_sibling(t, zs).start()
            hop(t, at(-4), 2, 0).wait_recv()
            hop(t, at(-4), -2, 1).wait_recv()
            to_sibling(t, at(-4)).start()

    def all_here(t):
        for s in range(nz):
            zs = at(s)
            slot = kv[t].at[2 * zs + 1 - k]
            remote(slot, slot, sib_send.at[t, zs], sib_recv.at[t, zs], sibling).wait_recv()

    load_k.wait()
    direct(0)

    def group(s):
        gg = lax.rem(g + s, ng)
        xx = lax.div(gg, 2)
        kk = lax.rem(gg, 2)
        return gg, xx, kk, {"dp": y * nx + xx, "ctx": 2 * z + kk}

    def columns_to(s):
        gg, xx, kk, device = group(s)
        return remote(x_out.at[gg], xg.at[g], xg_send.at[gg], xg_recv.at[g], device)

    load_x.wait()
    load_w.wait()
    v_all[c] = dot(x_v[...], w_v[...]).astype(jnp.bfloat16)
    for gg in range(ng):
        for i in range(yc):
            column = (((gg % 2) * yc + i) * nx + gg // 2) * BLOCK
            x_out[gg, i] = x_v[:, column : column + BLOCK]
    for s in range(1, ng):
        columns_to(s).start()

    load_q.wait()
    load_gc.wait()
    for h in range(heads):
        part = q_v[:, h * BLOCK : (h + 1) * BLOCK]
        rows = slice((h % 2) * BLOCK, (h % 2 + 1) * BLOCK)
        qn[h // 2, rows, :] = part
        qt[h // 2, :, rows] = part.T
        gcn[h // 2, rows, :] = gc_v[:, h * BLOCK : (h + 1) * BLOCK]

    relay(0)
    direct(1)

    block = ord_s[0, c]
    first = jnp.maximum(block - (wb - 1), 0)
    query_pos = block * BLOCK + lax.broadcasted_iota(jnp.int32, (1, BLOCK), 1)
    low = jnp.zeros((1, BLOCK), jnp.int32)
    end = jnp.int32(0)
    for i in range(len_s.shape[1]):
        end = end + len_s[0, i]
        low = jnp.where(query_pos >= end, end, low)
    key_pos = first * BLOCK + lax.broadcasted_iota(jnp.int32, (span, BLOCK), 0)
    bias[...] = jnp.where((key_pos >= low) & (key_pos <= query_pos), 0.0, NEG)
    kacc[...] = jnp.zeros_like(kacc)
    vacc[...] = jnp.zeros_like(vacc)
    for t in range(2):
        for i in range(pb + nc):
            if i < pb or i >= pb + wb:
                pad[t, i] = jnp.zeros((BLOCK, BLOCK), jnp.bfloat16)
    for h in range(heads):
        rows = slice((h % 2) * BLOCK, (h % 2 + 1) * BLOCK)
        gct[h // 2, :, rows] = gc_v[:, h * BLOCK : (h + 1) * BLOCK].T

    settle(0)
    all_here(0)

    for i in range(wb):
        kw[i * BLOCK : (i + 1) * BLOCK, :] = k_all[first + i]
    log_scale = score_scale * math.log2(math.e)

    def weigh(p, carry):
        scores = dot(kw[...], qt[p]) + jnp.concatenate([bias[...], bias[...]], axis=1)
        row_max = jnp.max(scores, axis=0, keepdims=True)
        exp_scores = jnp.exp2(scores * log_scale - row_max * log_scale)
        weights = (exp_scores * (1.0 / jnp.sum(exp_scores, axis=0, keepdims=True))).astype(
            jnp.bfloat16
        )
        wt[p] = weights
        vacc[...] += dot(weights, gcn[p])
        return carry

    lax.fori_loop(0, pairs // 2, weigh, 0)
    relay(1)
    lax.fori_loop(pairs // 2, pairs, weigh, 0)

    def half(t):
        return remote(sib_out.at[t], sib_in.at[t], half_send.at[t], half_recv.at[t], sibling)

    def swap_halves(t, acc, factor):
        for i in range(wb):
            pad[t, pb + i] = (acc[i * BLOCK : (i + 1) * BLOCK, :] * factor).astype(jnp.bfloat16)
        for zs in range(nz):
            sib_out[t, zs] = pad[t, pb + 2 * zs + 1 - k - first]
        half(t).start()

    def scatter(t, s):
        return remote(
            rs_out.at[t, at(s)], rs_in.at[t, z], rs_send.at[t, at(s)], rs_recv.at[t, z],
            {"ctx": 2 * at(s) + k},
        )

    def scatter_sums(t):
        half(t).wait_recv()
        for zs in range(nz):
            both = pad[t, pb + 2 * zs + k - first].astype(jnp.float32) + sib_in[t, zs].astype(
                jnp.float32
            )
            rs_out[t, zs] = both.astype(jnp.bfloat16)
        for s in sorted(range(1, nz), key=lambda s: -min(s, nz - s)):
            scatter(t, s).start()

    def gathered(t):
        total = rs_out[t, z].astype(jnp.float32)
        for s in sorted(range(1, nz), key=lambda s: min(s, nz - s)):
            zs = at(s)
            remote(
                rs_out.at[t, zs], rs_in.at[t, zs], rs_send.at[t, zs], rs_recv.at[t, zs],
                {"ctx": 2 * zs + k},
            ).wait_recv()
            total += rs_in[t, zs].astype(jnp.float32)
        return total.astype(jnp.bfloat16)

    swap_halves(1, vacc, 1.0)
    settle(1)
    scatter_sums(1)

    for i in range(wb):
        kwt[:, i * BLOCK : (i + 1) * BLOCK] = kw[i * BLOCK : (i + 1) * BLOCK, :].T
    all_here(1)
    for i in range(wb):
        value_block = v_all[first + i]
        vw[i * BLOCK : (i + 1) * BLOCK, :] = value_block
        vwt[:, i * BLOCK : (i + 1) * BLOCK] = value_block.T

    def attend(p, carry):
        weights = wt[p]
        turned = gct[p]
        context = dot(vwt[...], weights).astype(jnp.bfloat16)
        delta = jnp.sum(
            turned.astype(jnp.float32) * context.astype(jnp.float32), axis=0, keepdims=True
        )
        grad_prob = dot(vw[...], turned)
        grad_scores = (weights.astype(jnp.float32) * (grad_prob - delta)).astype(jnp.bfloat16)
        grad_query = (dot(kwt[...], grad_scores) * score_scale).astype(jnp.bfloat16)
        kacc[...] += dot(grad_scores, qn[p])
        for i in range(2):
            columns = pl.ds(pl.multiple_of((2 * p + i) * BLOCK, BLOCK), BLOCK)
            lanes = slice(i * BLOCK, (i + 1) * BLOCK)
            ctx_v[:, columns] = context[:, lanes].T
            gq_v[:, columns] = grad_query[:, lanes].T
        return carry

    lax.fori_loop(0, pairs, attend, 0)
    store_ctx = pltpu.make_async_copy(ctx_v, ctx_o, store_sem.at[0])
    store_gq = pltpu.make_async_copy(gq_v, gq_o, store_sem.at[1])
    swap_halves(0, kacc, score_scale)
    store_ctx.start()
    store_gq.start()

    for s in range(1, ng):
        gg, xx, kk, device = group(s)
        remote(xg.at[gg], xg.at[gg], xg_send.at[gg], xg_recv.at[gg], device).wait_recv()
    xg[g] = x_out[g]
    for gg in range(ng):
        for i in range(yc):
            xgt[i, :, gg * BLOCK : (gg + 1) * BLOCK] = xg[gg, i].T

    gvg[g] = gathered(1)

    def share(s):
        gg, xx, kk, device = group(s)
        return remote(gvg.at[g], gvg.at[g], gv_send.at[gg], gv_recv.at[g], device)

    for s in range(1, ng):
        share(s).start()
    scatter_sums(0)
    store_gv = pltpu.make_async_copy(gvg.at[g], gv_o, store_sem.at[2])
    store_gv.start()
    for s in range(1, ng):
        gg, xx, kk, device = group(s)
        remote(gvg.at[gg], gvg.at[gg], gv_send.at[gg], gv_recv.at[gg], device).wait_recv()

    group_rows = gvg[...].reshape(ng * BLOCK, BLOCK)
    source_core = lax.div(y, yc)

    def to_y(i, kk):
        yy = k * yc + i
        return (yy != y) | (kk != k), remote(
            p_out.at[i, kk], p_in.at[y], p_send.at[i, kk], p_recv.at[y],
            {"dp": yy * nx + x, "ctx": 2 * z + kk},
        )

    for i in range(yc):
        product = dot(xgt[i], group_rows).reshape(nz, 2, fr, BLOCK)
        for kk in range(2):
            p_out[i, kk] = product[:, kk].reshape(nz * fr, BLOCK).astype(jnp.bfloat16)
            away, copy = to_y(i, kk)
            pl.when(away)(copy.start)

    @pl.when(source_core == k)
    def _():
        p_in[y] = p_out[lax.rem(y, yc), k]

    total = jnp.zeros((nz * fr, BLOCK), jnp.float32)
    for s in range(ny):
        yy = lax.rem(y + s, ny)
        copy = remote(
            p_in.at[yy], p_in.at[yy], p_send.at[0, 0], p_recv.at[yy],
            {"dp": yy * nx + x, "ctx": 2 * z + 1 - k},
        )
        if s == 0:
            pl.when(source_core != k)(copy.wait_recv)
        else:
            copy.wait_recv()
        total += p_in[yy].astype(jnp.float32)
    r_v[...] = total

    def to_z(s):
        zs = at(s)
        rows = pl.ds(pl.multiple_of(zs * fr, fr), fr)
        return remote(
            r_v.at[rows], r_in.at[z], r_send.at[zs], r_recv.at[z], {"ctx": 2 * zs + k}
        )

    for s in sorted(range(1, nz), key=lambda s: -min(s, nz - s)):
        to_z(s).start()

    gkv_v[...] = gathered(0)
    store_gk = pltpu.make_async_copy(gkv_v, gk_o, store_sem.at[3])
    store_gk.start()

    total = r_v[pl.ds(pl.multiple_of(z * fr, fr), fr), :]
    for s in sorted(range(1, nz), key=lambda s: min(s, nz - s)):
        zs = at(s)
        remote(
            r_in.at[zs], r_in.at[zs], r_send.at[zs], r_recv.at[zs], {"ctx": 2 * zs + k}
        ).wait_recv()
        total += r_in[zs]
    gw_v[...] = total
    store_gw = pltpu.make_async_copy(gw_v, gw_o, store_sem.at[4])
    store_gw.start()

    for t in range(2):
        for s in near:
            hop(t, z, s).wait_send()
        for source, s in relays:
            hop(t, at(source), 2 * s, 0 if s > 0 else 1).wait_send()
            hop(t, at(source), s).wait_send()
        for zs in range(nz):
            to_sibling(t, zs).wait_send()
        half(t).wait_send()
        for s in range(1, nz):
            scatter(t, s).wait_send()
    for s in range(1, ng):
        columns_to(s).wait_send()
        share(s).wait_send()
    for i in range(yc):
        for kk in range(2):
            away, copy = to_y(i, kk)
            pl.when(away)(copy.wait_send)
    for s in range(1, nz):
        to_z(s).wait_send()

    for one in (store_ctx, store_gq, store_gv, store_gk, store_gw):
        one.wait()


def write_out(*refs):
    held, sems = refs[10:15], refs[15]
    for i in range(5):
        pltpu.make_async_copy(refs[i], held[i], sems.at[0, i]).start()
    for i in range(5):
        pltpu.make_async_copy(refs[i], held[i], sems.at[0, i]).wait()
        pltpu.make_async_copy(held[i], refs[5 + i], sems.at[1, i]).start()
    for i in range(5):
        pltpu.make_async_copy(held[i], refs[5 + i], sems.at[1, i]).wait()


def body(nx, ny, nz, queries, key_rows, x_rows, value_weight, grad_context, doc_lengths, block_order):
    rows, width = queries.shape[1:]
    features = x_rows.shape[2]
    heads = width // BLOCK
    nc = 2 * nz
    wb = nc // 2 + 1
    pb = nc - wb
    yc = ny // 2
    ng = 2 * nx
    fr = BLOCK // nc
    pairs = heads // 2
    span = wb * BLOCK
    bf16, f32 = jnp.bfloat16, jnp.float32
    sq = (BLOCK, BLOCK)
    anywhere = pl.BlockSpec(memory_space=pltpu.HBM)
    scalars = pl.BlockSpec(memory_space=pltpu.SMEM)
    dma = pltpu.SemaphoreType.DMA
    outs = pl.pallas_call(
        functools.partial(kernel, nx, ny, nz, heads),
        out_shape=(
            jax.ShapeDtypeStruct((rows, width), bf16),
            jax.ShapeDtypeStruct((rows, width), bf16),
            jax.ShapeDtypeStruct(sq, bf16),
            jax.ShapeDtypeStruct(sq, bf16),
            jax.ShapeDtypeStruct((fr, BLOCK), f32),
        ),
        in_specs=[anywhere] * 5 + [scalars] * 2,
        out_specs=(anywhere,) * 5,
        scratch_shapes=[
            pltpu.VMEM((rows, width), bf16),
            pltpu.VMEM((rows, width), bf16),
            pltpu.VMEM((rows, features), bf16),
            pltpu.VMEM((features, BLOCK), bf16),
            pltpu.VMEM((nc,) + sq, bf16),
            pltpu.VMEM((nc,) + sq, bf16),
            pltpu.VMEM((pairs, 2 * BLOCK, BLOCK), bf16),
            pltpu.VMEM((pairs, BLOCK, 2 * BLOCK), bf16),
            pltpu.VMEM((pairs, 2 * BLOCK, BLOCK), bf16),
            pltpu.VMEM((pairs, BLOCK, 2 * BLOCK), bf16),
            pltpu.VMEM((span, BLOCK), f32),
            pltpu.VMEM((span, BLOCK), bf16),
            pltpu.VMEM((span, BLOCK), bf16),
            pltpu.VMEM((BLOCK, span), bf16),
            pltpu.VMEM((BLOCK, span), bf16),
            pltpu.VMEM((pairs, span, 2 * BLOCK), bf16),
            pltpu.VMEM((span, BLOCK), f32),
            pltpu.VMEM((span, BLOCK), f32),
            pltpu.VMEM((2, pb + nc) + sq, bf16),
            pltpu.VMEM((2, nz) + sq, bf16),
            pltpu.VMEM((2, nz) + sq, bf16),
            pltpu.VMEM((2, nz) + sq, bf16),
            pltpu.VMEM((2, nz) + sq, bf16),
            pltpu.VMEM((rows, width), bf16),
            pltpu.VMEM((rows, width), bf16),
            pltpu.VMEM(sq, bf16),
            pltpu.VMEM((ng, yc) + sq, bf16),
            pltpu.VMEM((ng, yc) + sq, bf16),
            pltpu.VMEM((yc, BLOCK, ng * BLOCK), bf16),
            pltpu.VMEM((ng,) + sq, bf16),
            pltpu.VMEM((yc, 2, nz * fr, BLOCK), bf16),
            pltpu.VMEM((ny, nz * fr, BLOCK), bf16),
            pltpu.VMEM((nz * fr, BLOCK), f32),
            pltpu.VMEM((nz, fr, BLOCK), f32),
            pltpu.VMEM((fr, BLOCK), f32),
            dma((5,)),
            dma((5,)),
            dma((2, nz, 5)),
            dma((2, nz)),
            dma((2, 2)),
            dma((2, 2)),
            dma((2, nz)),
            dma((2, nz)),
            dma((2,)),
            dma((2,)),
            dma((2, nz)),
            dma((2, nz)),
            dma((ng,)),
            dma((ng,)),
            dma((ng,)),
            dma((ng,)),
            dma((yc, 2)),
            dma((ny,)),
            dma((nz,)),
            dma((nz,)),
        ],
        compiler_params=pltpu.CompilerParams(
            collective_id=0, has_side_effects=True, vmem_limit_bytes=VMEM_LIMIT
        ),
        name="attention_core",
    )(
        queries[0], key_rows[0], x_rows[0], value_weight, grad_context[0], doc_lengths, block_order
    )
    context, grad_queries, grad_keys, grad_values, grad_weight = pl.pallas_call(
        write_out,
        out_shape=tuple(jax.ShapeDtypeStruct(one.shape, one.dtype) for one in outs),
        in_specs=[anywhere] * 5,
        out_specs=(anywhere,) * 5,
        scratch_shapes=[pltpu.VMEM(one.shape, one.dtype) for one in outs] + [dma((2, 5))],
        compiler_params=pltpu.CompilerParams(vmem_limit_bytes=VMEM_LIMIT),
        name="write_out",
    )(*outs)
    return (context[None], grad_queries[None], grad_keys[None], grad_values[None], grad_weight)


def solution(mesh, sizes=(4, 8, 8)):
    placed = (
        P("dp", "ctx", None),
        P("dp", "ctx", None),
        P("dp", "ctx", None),
        P(),
        P("dp", "ctx", None),
        P("dp", None),
        P("dp", None),
    )
    return jax.shard_map(
        functools.partial(body, *sizes),
        mesh=mesh,
        in_specs=placed,
        out_specs=(
            P("dp", "ctx", None),
            P("dp", "ctx", None),
            P("dp", "ctx", None),
            P("dp", "ctx", None),
            P(("dp", "ctx"), None),
        ),
        check_vma=False,
    )
```

```python
import functools
import math

import jax
import jax.numpy as jnp
from jax import lax
from jax.experimental import pallas as pl
from jax.experimental.pallas import tpu as pltpu
from jax.sharding import PartitionSpec as P

BLOCK = 128
MESH = pl.DeviceIdType.MESH
NEG = -1e30
VMEM_LIMIT = 60 * 1024 * 1024


def remote(src, dst, send_sem, recv_sem, device):
    return pltpu.make_async_remote_copy(
        src_ref=src,
        dst_ref=dst,
        send_sem=send_sem,
        recv_sem=recv_sem,
        device_id=device,
        device_id_type=MESH,
    )


def dot(a, b):
    return jnp.dot(a, b, preferred_element_type=jnp.float32)


def kernel(
    nx, ny, nz, heads,
    q_hbm, k_hbm, x_hbm, w_hbm, gc_hbm, len_s, ord_s,
    ctx_o, gq_o, gk_o, gv_o, gw_o,
    q_v, gc_v, x_v, w_v, k_all, v_all, qn, qt, gcn, gct, bias, kw, vw, kwt, vwt,
    wt, kacc, vacc, pad, sib_out, sib_in, rs_out, rs_in, ctx_v, gq_v, gkv_v,
    x_out, xg, xgt, gvg, p_out, p_in, r_v, r_in, gw_v,
    ready, load_sem, store_sem, hop_send, hop_recv, sib_send, sib_recv,
    half_send, half_recv, rs_send, rs_recv, xg_send, xg_recv,
    gv_send, gv_recv, p_send, p_recv, r_send, r_recv,
):
    nc = 2 * nz
    wb = nc // 2 + 1
    pb = nc - wb
    yc = ny // 2
    ng = 2 * nx
    fr = BLOCK // nc
    pairs = heads // 2
    span = wb * BLOCK
    d = lax.axis_index("dp")
    c = lax.axis_index("ctx")
    y = lax.div(d, nx)
    x = lax.rem(d, nx)
    z = lax.div(c, 2)
    k = lax.rem(c, 2)
    g = 2 * x + k
    kv = (k_all, v_all)
    score_scale = 1.0 / math.sqrt(BLOCK)

    sibling = {"ctx": 2 * z + 1 - k}

    def load(src, dst, n):
        return pltpu.make_async_copy(src, dst, load_sem.at[n])

    load_k = load(k_hbm, k_all.at[c], 0)
    load_x = load(x_hbm, x_v, 1)
    load_w = load(w_hbm, w_v, 2)
    load_q = load(q_hbm, q_v, 3)
    load_gc = load(gc_hbm, gc_v, 4)
    for one in (load_k, load_x, load_w, load_q, load_gc):
        one.start()

    barrier = pltpu.get_barrier_semaphore()

    def around(n, most):
        return sorted({s % n for s in range(-most, most + 1)} - {0})

    planar = [{"dp": y * nx + lax.rem(x + s, nx)} for s in around(nx, 1)]
    planar += [{"dp": lax.rem(y + s, ny) * nx + x} for s in around(ny, 1)]
    planar.append(sibling)
    partners = planar + [{"ctx": 2 * lax.rem(z + s, nz) + k} for s in around(nz, 2)]
    for device in partners:
        pl.semaphore_signal(barrier, 1, device_id=device, device_id_type=MESH)
    pl.semaphore_wait(barrier, len(partners))

    def tell(n):
        for device in planar:
            pl.semaphore_signal(ready.at[n], 1, device_id=device, device_id_type=MESH)

    def hear(n):
        pl.semaphore_wait(ready.at[n], len(planar))


    def at(s):
        return lax.rem(z + (s + 2 * nz), nz)

    def hop(t, zs, s, kind, part=None):
        slot = kv[t].at[2 * zs + k]
        if part is not None:
            slot = slot.at[pl.ds(part * (BLOCK // 2), BLOCK // 2)]
        return remote(slot, slot, hop_send.at[t], hop_recv.at[t, kind], {"ctx": 2 * at(s) + k})

    def hops(t, kind, count):
        slots = kv[t].at[pl.ds(0, count)]
        return remote(slots, slots, hop_send.at[t], hop_recv.at[t, kind], sibling)

    def to_sibling(t, zs):
        slot = kv[t].at[2 * zs + k]
        return remote(slot, slot, sib_send.at[t], sib_recv.at[t], sibling)

    def all_siblings(t):
        slots = kv[t].at[pl.ds(0, nz)]
        return remote(slots, slots, sib_send.at[t], sib_recv.at[t], sibling)

    relayed = nz == 8
    close = (1, -1) if nz > 2 else (1,)
    if nz == 4:
        close = (2, 1, -1)

    def direct(t):
        if relayed:
            hop(t, z, 2, 0).start()
            hop(t, z, -2, 1).start()
        for s in close:
            hop(t, z, s, 2).start()
        to_sibling(t, z).start()

    def relay(t):
        if relayed:
            for kind, s in ((0, 1), (1, -1)):
                zs = at(-2 * s)
                hops(t, kind, 1).wait_recv()
                hop(t, zs, 2 * s, 3, kind).start()
                hop(t, zs, s, 3).start()
                to_sibling(t, zs).start()
        hops(t, 2, len(close)).wait_recv()
        for s in close:
            to_sibling(t, at(-s)).start()

    def settle(t):
        if relayed:
            hops(t, 3, 3).wait_recv()
            for s in (3, -3, 4):
                to_sibling(t, at(s)).start()

    load_k.wait()
    direct(0)
    tell(0)

    def group(s):
        gg = lax.rem(g + s, ng)
        xx = lax.div(gg, 2)
        kk = lax.rem(gg, 2)
        return gg, xx, kk, {"dp": y * nx + xx, "ctx": 2 * z + kk}

    def columns_to(s):
        gg, xx, kk, device = group(s)
        return remote(x_out.at[gg], xg.at[g], xg_send, xg_recv, device)

    def all_columns():
        return remote(x_out.at[pl.ds(0, ng - 1)], xg.at[pl.ds(0, ng - 1)], xg_send, xg_recv, sibling)

    load_x.wait()
    load_w.wait()
    v_all[c] = dot(x_v[...], w_v[...]).astype(jnp.bfloat16)
    for gg in range(ng):
        for i in range(yc):
            column = (((gg % 2) * yc + i) * nx + gg // 2) * BLOCK
            x_out[gg, i] = x_v[:, column : column + BLOCK]
    load_q.wait()
    load_gc.wait()
    for h in range(heads):
        part = q_v[:, h * BLOCK : (h + 1) * BLOCK]
        rows = slice((h % 2) * BLOCK, (h % 2 + 1) * BLOCK)
        qn[h // 2, rows, :] = part
        qt[h // 2, :, rows] = part.T
        gcn[h // 2, rows, :] = gc_v[:, h * BLOCK : (h + 1) * BLOCK]

    relay(0)
    direct(1)
    hear(0)
    tell(1)

    block = ord_s[0, c]
    first = jnp.maximum(block - (wb - 1), 0)
    query_pos = block * BLOCK + lax.broadcasted_iota(jnp.int32, (1, BLOCK), 1)
    low = jnp.zeros((1, BLOCK), jnp.int32)
    end = jnp.int32(0)
    for i in range(len_s.shape[1]):
        end = end + len_s[0, i]
        low = jnp.where(query_pos >= end, end, low)
    key_pos = first * BLOCK + lax.broadcasted_iota(jnp.int32, (span, BLOCK), 0)
    bias[...] = jnp.where((key_pos >= low) & (key_pos <= query_pos), 0.0, NEG)
    kacc[...] = jnp.zeros_like(kacc)
    vacc[...] = jnp.zeros_like(vacc)
    for t in range(2):
        for i in range(pb + nc):
            if i < pb or i >= pb + wb:
                pad[t, i] = jnp.zeros((BLOCK, BLOCK), jnp.bfloat16)
    for h in range(heads):
        rows = slice((h % 2) * BLOCK, (h % 2 + 1) * BLOCK)
        gct[h // 2, :, rows] = gc_v[:, h * BLOCK : (h + 1) * BLOCK].T

    settle(0)
    hear(1)
    tell(2)
    for s in range(1, ng):
        columns_to(s).start()
    all_siblings(0).wait_recv()

    for i in range(wb):
        kw[i * BLOCK : (i + 1) * BLOCK, :] = k_all[first + i]
    log_scale = score_scale * math.log2(math.e)

    def weigh(p, carry):
        scores = dot(kw[...], qt[p]) + jnp.concatenate([bias[...], bias[...]], axis=1)
        row_max = jnp.max(scores, axis=0, keepdims=True)
        exp_scores = jnp.exp2(scores * log_scale - row_max * log_scale)
        weights = (exp_scores * (1.0 / jnp.sum(exp_scores, axis=0, keepdims=True))).astype(
            jnp.bfloat16
        )
        wt[p] = weights
        vacc[...] += dot(weights, gcn[p])
        return carry

    lax.fori_loop(0, pairs // 2, weigh, 0, unroll=True)
    relay(1)
    lax.fori_loop(pairs // 2, pairs, weigh, 0, unroll=True)

    def half(t):
        return remote(sib_out.at[t], sib_in.at[t], half_send.at[t], half_recv.at[t], sibling)

    def swap_halves(t, acc, factor):
        for i in range(wb):
            pad[t, pb + i] = (acc[i * BLOCK : (i + 1) * BLOCK, :] * factor).astype(jnp.bfloat16)
        for zs in range(nz):
            sib_out[t, zs] = pad[t, pb + 2 * zs + 1 - k - first]
        half(t).start()

    def scatter(t, s):
        return remote(
            rs_out.at[t, at(s)], rs_in.at[t, z], rs_send.at[t], rs_recv.at[t],
            {"ctx": 2 * at(s) + k},
        )

    def all_scattered(t):
        return remote(
            rs_out.at[t, pl.ds(0, nz - 1)], rs_in.at[t, pl.ds(0, nz - 1)],
            rs_send.at[t], rs_recv.at[t], sibling,
        )

    def scatter_sums(t):
        half(t).wait_recv()
        for zs in range(nz):
            both = pad[t, pb + 2 * zs + k - first].astype(jnp.float32) + sib_in[t, zs].astype(
                jnp.float32
            )
            rs_out[t, zs] = both.astype(jnp.bfloat16)
        for s in sorted(range(1, nz), key=lambda s: -min(s, nz - s)):
            scatter(t, s).start()

    def gathered(t):
        all_scattered(t).wait_recv()
        total = rs_out[t, z].astype(jnp.float32)
        for s in range(1, nz):
            total += rs_in[t, at(s)].astype(jnp.float32)
        return total.astype(jnp.bfloat16)

    swap_halves(1, vacc, 1.0)
    settle(1)
    scatter_sums(1)
    hear(2)
    tell(3)

    for i in range(wb):
        kwt[:, i * BLOCK : (i + 1) * BLOCK] = kw[i * BLOCK : (i + 1) * BLOCK, :].T
    all_siblings(1).wait_recv()
    for i in range(wb):
        value_block = v_all[first + i]
        vw[i * BLOCK : (i + 1) * BLOCK, :] = value_block
        vwt[:, i * BLOCK : (i + 1) * BLOCK] = value_block.T

    def attend(p, carry):
        weights = wt[p]
        turned = gct[p]
        context = dot(vwt[...], weights).astype(jnp.bfloat16)
        delta = jnp.sum(
            turned.astype(jnp.float32) * context.astype(jnp.float32), axis=0, keepdims=True
        )
        grad_prob = dot(vw[...], turned)
        grad_scores = (weights.astype(jnp.float32) * (grad_prob - delta)).astype(jnp.bfloat16)
        grad_query = (dot(kwt[...], grad_scores) * score_scale).astype(jnp.bfloat16)
        kacc[...] += dot(grad_scores, qn[p])
        for i in range(2):
            columns = pl.ds(pl.multiple_of((2 * p + i) * BLOCK, BLOCK), BLOCK)
            lanes = slice(i * BLOCK, (i + 1) * BLOCK)
            ctx_v[:, columns] = context[:, lanes].T
            gq_v[:, columns] = grad_query[:, lanes].T
        return carry

    lax.fori_loop(0, pairs, attend, 0, unroll=True)
    store_ctx = pltpu.make_async_copy(ctx_v, ctx_o, store_sem.at[0])
    store_gq = pltpu.make_async_copy(gq_v, gq_o, store_sem.at[1])
    swap_halves(0, kacc, score_scale)
    store_ctx.start()
    store_gq.start()

    gvg[g] = gathered(1)

    def share(s):
        gg, xx, kk, device = group(s)
        return remote(gvg.at[g], gvg.at[g], gv_send, gv_recv, device)

    def all_shared():
        return remote(gvg.at[pl.ds(0, ng - 1)], gvg.at[pl.ds(0, ng - 1)], gv_send, gv_recv, sibling)

    for s in range(1, ng):
        share(s).start()
    scatter_sums(0)

    all_columns().wait_recv()
    xg[g] = x_out[g]
    for gg in range(ng):
        for i in range(yc):
            xgt[i, :, gg * BLOCK : (gg + 1) * BLOCK] = xg[gg, i].T
    hear(3)

    store_gv = pltpu.make_async_copy(gvg.at[g], gv_o, store_sem.at[2])
    store_gv.start()
    all_shared().wait_recv()

    group_rows = gvg[...].reshape(ng * BLOCK, BLOCK)
    source_core = lax.div(y, yc)

    def to_y(i, kk):
        yy = k * yc + i
        return (yy != y) | (kk != k), remote(
            p_out.at[2 * i + kk], p_in.at[y], p_send, p_recv,
            {"dp": yy * nx + x, "ctx": 2 * z + kk},
        )

    def all_y(count):
        return remote(p_out.at[pl.ds(0, count)], p_in.at[pl.ds(0, count)], p_send, p_recv, sibling)

    for i in range(yc):
        product = dot(xgt[i], group_rows).reshape(nz, 2, fr, BLOCK)
        for kk in range(2):
            p_out[2 * i + kk] = product[:, kk].reshape(nz * fr, BLOCK).astype(jnp.bfloat16)
            away, copy = to_y(i, kk)
            pl.when(away)(copy.start)

    @pl.when(source_core == k)
    def _():
        all_y(ny - 1).wait_recv()
        p_in[y] = p_out[2 * lax.rem(y, yc) + k]

    @pl.when(source_core != k)
    def _():
        all_y(ny).wait_recv()

    r_v[...] = jnp.sum(p_in[...].astype(jnp.float32), axis=0)

    def to_z(s):
        zs = at(s)
        rows = pl.ds(pl.multiple_of(zs * fr, fr), fr)
        return remote(
            r_v.at[rows], r_in.at[z], r_send, r_recv, {"ctx": 2 * zs + k}
        )

    for s in sorted(range(1, nz), key=lambda s: -min(s, nz - s)):
        to_z(s).start()

    gkv_v[...] = gathered(0)
    store_gk = pltpu.make_async_copy(gkv_v, gk_o, store_sem.at[3])
    store_gk.start()

    def all_z():
        return remote(
            r_in.at[pl.ds(0, nz - 1)], r_in.at[pl.ds(0, nz - 1)], r_send, r_recv, sibling
        )

    all_z().wait_recv()
    total = r_v[pl.ds(pl.multiple_of(z * fr, fr), fr), :]
    for s in range(1, nz):
        total += r_in[at(s)]
    gw_v[...] = total
    store_gw = pltpu.make_async_copy(gw_v, gw_o, store_sem.at[4])
    store_gw.start()

    for t in range(2):
        hops(t, 0, nz - 1).wait_send()
        all_siblings(t).wait_send()
        half(t).wait_send()
        all_scattered(t).wait_send()
    all_columns().wait_send()
    all_shared().wait_send()
    pl.when(source_core == k)(all_y(2 * yc - 1).wait_send)
    pl.when(source_core != k)(all_y(2 * yc).wait_send)
    all_z().wait_send()

    for one in (store_ctx, store_gq, store_gv, store_gk, store_gw):
        one.wait()


def write_out(*refs):
    held, sems = refs[10:15], refs[15]
    for i in range(5):
        pltpu.make_async_copy(refs[i], held[i], sems.at[0, i]).start()
    for i in range(5):
        pltpu.make_async_copy(refs[i], held[i], sems.at[0, i]).wait()
        pltpu.make_async_copy(held[i], refs[5 + i], sems.at[1, i]).start()
    for i in range(5):
        pltpu.make_async_copy(held[i], refs[5 + i], sems.at[1, i]).wait()


def body(nx, ny, nz, queries, key_rows, x_rows, value_weight, grad_context, doc_lengths, block_order):
    rows, width = queries.shape[1:]
    features = x_rows.shape[2]
    heads = width // BLOCK
    nc = 2 * nz
    wb = nc // 2 + 1
    pb = nc - wb
    yc = ny // 2
    ng = 2 * nx
    fr = BLOCK // nc
    pairs = heads // 2
    span = wb * BLOCK
    bf16, f32 = jnp.bfloat16, jnp.float32
    sq = (BLOCK, BLOCK)
    anywhere = pl.BlockSpec(memory_space=pltpu.HBM)
    scalars = pl.BlockSpec(memory_space=pltpu.SMEM)
    dma = pltpu.SemaphoreType.DMA
    outs = pl.pallas_call(
        functools.partial(kernel, nx, ny, nz, heads),
        out_shape=(
            jax.ShapeDtypeStruct((rows, width), bf16),
            jax.ShapeDtypeStruct((rows, width), bf16),
            jax.ShapeDtypeStruct(sq, bf16),
            jax.ShapeDtypeStruct(sq, bf16),
            jax.ShapeDtypeStruct((fr, BLOCK), f32),
        ),
        in_specs=[anywhere] * 5 + [scalars] * 2,
        out_specs=(anywhere,) * 5,
        scratch_shapes=[
            pltpu.VMEM((rows, width), bf16),
            pltpu.VMEM((rows, width), bf16),
            pltpu.VMEM((rows, features), bf16),
            pltpu.VMEM((features, BLOCK), bf16),
            pltpu.VMEM((nc,) + sq, bf16),
            pltpu.VMEM((nc,) + sq, bf16),
            pltpu.VMEM((pairs, 2 * BLOCK, BLOCK), bf16),
            pltpu.VMEM((pairs, BLOCK, 2 * BLOCK), bf16),
            pltpu.VMEM((pairs, 2 * BLOCK, BLOCK), bf16),
            pltpu.VMEM((pairs, BLOCK, 2 * BLOCK), bf16),
            pltpu.VMEM((span, BLOCK), f32),
            pltpu.VMEM((span, BLOCK), bf16),
            pltpu.VMEM((span, BLOCK), bf16),
            pltpu.VMEM((BLOCK, span), bf16),
            pltpu.VMEM((BLOCK, span), bf16),
            pltpu.VMEM((pairs, span, 2 * BLOCK), bf16),
            pltpu.VMEM((span, BLOCK), f32),
            pltpu.VMEM((span, BLOCK), f32),
            pltpu.VMEM((2, pb + nc) + sq, bf16),
            pltpu.VMEM((2, nz) + sq, bf16),
            pltpu.VMEM((2, nz) + sq, bf16),
            pltpu.VMEM((2, nz) + sq, bf16),
            pltpu.VMEM((2, nz) + sq, bf16),
            pltpu.VMEM((rows, width), bf16),
            pltpu.VMEM((rows, width), bf16),
            pltpu.VMEM(sq, bf16),
            pltpu.VMEM((ng, yc) + sq, bf16),
            pltpu.VMEM((ng, yc) + sq, bf16),
            pltpu.VMEM((yc, BLOCK, ng * BLOCK), bf16),
            pltpu.VMEM((ng,) + sq, bf16),
            pltpu.VMEM((2 * yc, nz * fr, BLOCK), bf16),
            pltpu.VMEM((ny, nz * fr, BLOCK), bf16),
            pltpu.VMEM((nz * fr, BLOCK), f32),
            pltpu.VMEM((nz, fr, BLOCK), f32),
            pltpu.VMEM((fr, BLOCK), f32),
            pltpu.SemaphoreType.REGULAR((4,)),
            dma((5,)),
            dma((5,)),
            dma((2,)),
            dma((2, 4)),
            dma((2,)),
            dma((2,)),
            dma((2,)),
            dma((2,)),
            dma((2,)),
            dma((2,)),
        ]
        + [dma] * 8,
        compiler_params=pltpu.CompilerParams(
            collective_id=0, has_side_effects=True, vmem_limit_bytes=VMEM_LIMIT
        ),
        name="attention_core",
    )(
        queries[0], key_rows[0], x_rows[0], value_weight, grad_context[0], doc_lengths, block_order
    )
    context, grad_queries, grad_keys, grad_values, grad_weight = pl.pallas_call(
        write_out,
        out_shape=tuple(jax.ShapeDtypeStruct(one.shape, one.dtype) for one in outs),
        in_specs=[anywhere] * 5,
        out_specs=(anywhere,) * 5,
        scratch_shapes=[pltpu.VMEM(one.shape, one.dtype) for one in outs] + [dma((2, 5))],
        compiler_params=pltpu.CompilerParams(vmem_limit_bytes=VMEM_LIMIT),
        name="write_out",
    )(*outs)
    return (context[None], grad_queries[None], grad_keys[None], grad_values[None], grad_weight)


def solution(mesh, sizes=(4, 8, 8)):
    placed = (
        P("dp", "ctx", None),
        P("dp", "ctx", None),
        P("dp", "ctx", None),
        P(),
        P("dp", "ctx", None),
        P("dp", None),
        P("dp", None),
    )
    return jax.shard_map(
        functools.partial(body, *sizes),
        mesh=mesh,
        in_specs=placed,
        out_specs=(
            P("dp", "ctx", None),
            P("dp", "ctx", None),
            P("dp", "ctx", None),
            P("dp", "ctx", None),
            P(("dp", "ctx"), None),
        ),
        check_vma=False,
    )
```

```python
import functools
import math

import jax
import jax.numpy as jnp
from jax import lax
from jax.experimental import pallas as pl
from jax.experimental.pallas import tpu as pltpu
from jax.sharding import PartitionSpec as P

BLOCK = 128
MESH = pl.DeviceIdType.MESH
NEG = -1e30
VMEM_LIMIT = 60 * 1024 * 1024


def remote(src, dst, send_sem, recv_sem, device):
    return pltpu.make_async_remote_copy(
        src_ref=src,
        dst_ref=dst,
        send_sem=send_sem,
        recv_sem=recv_sem,
        device_id=device,
        device_id_type=MESH,
    )


def dot(a, b):
    return jnp.dot(a, b, preferred_element_type=jnp.float32)


def kernel(
    nx, ny, nz, heads,
    q_hbm, k_hbm, x_hbm, w_hbm, gc_hbm, len_s, ord_s,
    ctx_o, gq_o, gk_o, gv_o, gw_o,
    q_v, gc_v, x_v, w_v, k_all, v_all, qn, qt, gcn, gct, bias, kw, vw, kwt, vwt,
    wt, kacc, vacc, pad, sib_out, sib_in, rs_out, rs_in, ctx_v, gq_v, gkv_v,
    x_out, xg, xgt, gvg, p_out, p_in, r_v, r_in, gw_v,
    ready, load_sem, store_sem, hop_send, hop_recv, sib_send, sib_recv,
    half_send, half_recv, rs_send, rs_recv, xg_send, xg_recv,
    gv_send, gv_recv, p_send, p_recv, r_send, r_recv,
):
    nc = 2 * nz
    wb = nc // 2 + 1
    pb = nc - wb
    yc = ny // 2
    ng = 2 * nx
    fr = BLOCK // nc
    pairs = heads // 2
    span = wb * BLOCK
    d = lax.axis_index("dp")
    c = lax.axis_index("ctx")
    y = lax.div(d, nx)
    x = lax.rem(d, nx)
    z = lax.div(c, 2)
    k = lax.rem(c, 2)
    g = 2 * x + k
    kv = (k_all, v_all)
    score_scale = 1.0 / math.sqrt(BLOCK)

    sibling = {"ctx": 2 * z + 1 - k}

    def load(src, dst, n):
        return pltpu.make_async_copy(src, dst, load_sem.at[n])

    load_k = load(k_hbm, k_all.at[c], 0)
    load_x = load(x_hbm, x_v, 1)
    load_w = load(w_hbm, w_v, 2)
    load_q = load(q_hbm, q_v, 3)
    load_gc = load(gc_hbm, gc_v, 4)
    load_k.start()

    barrier = pltpu.get_barrier_semaphore()

    def around(n, most):
        return sorted({s % n for s in range(-most, most + 1)} - {0})

    planar = [{"dp": y * nx + lax.rem(x + s, nx)} for s in around(nx, 1)]
    planar += [{"dp": lax.rem(y + s, ny) * nx + x} for s in around(ny, 1)]
    planar.append(sibling)
    partners = planar + [{"ctx": 2 * lax.rem(z + s, nz) + k} for s in around(nz, 2)]
    for device in partners:
        pl.semaphore_signal(barrier, 1, device_id=device, device_id_type=MESH)
    for one in (load_q, load_x, load_w, load_gc):
        one.start()
    pl.semaphore_wait(barrier, len(partners))

    def tell(n):
        for device in planar:
            pl.semaphore_signal(ready.at[n], 1, device_id=device, device_id_type=MESH)

    def hear(n):
        pl.semaphore_wait(ready.at[n], len(planar))


    def at(s):
        return lax.rem(z + (s + 2 * nz), nz)

    def hop(t, zs, s, kind, part=None):
        slot = kv[t].at[2 * zs + k]
        if part is not None:
            slot = slot.at[pl.ds(part * (BLOCK // 2), BLOCK // 2)]
        return remote(slot, slot, hop_send.at[t], hop_recv.at[t, kind], {"ctx": 2 * at(s) + k})

    def hops(t, kind, count):
        slots = kv[t].at[pl.ds(0, count)]
        return remote(slots, slots, hop_send.at[t], hop_recv.at[t, kind], sibling)

    def to_sibling(t, zs):
        slot = kv[t].at[2 * zs + k]
        return remote(slot, slot, sib_send.at[t], sib_recv.at[t], sibling)

    def all_siblings(t):
        slots = kv[t].at[pl.ds(0, nz)]
        return remote(slots, slots, sib_send.at[t], sib_recv.at[t], sibling)

    relayed = nz == 8
    close = (1, -1) if nz > 2 else (1,)
    if nz == 4:
        close = (2, 1, -1)

    def direct(t):
        if relayed:
            hop(t, z, 2, 0).start()
            hop(t, z, -2, 1).start()
        for s in close:
            hop(t, z, s, 2).start()
        to_sibling(t, z).start()

    def relay(t):
        if relayed:
            for kind, s in ((0, 1), (1, -1)):
                zs = at(-2 * s)
                hops(t, kind, 1).wait_recv()
                hop(t, zs, 2 * s, 3, kind).start()
                hop(t, zs, s, 3).start()
                to_sibling(t, zs).start()
        hops(t, 2, len(close)).wait_recv()
        for s in close:
            to_sibling(t, at(-s)).start()

    def settle(t):
        if relayed:
            hops(t, 3, 3).wait_recv()
            for s in (3, -3, 4):
                to_sibling(t, at(s)).start()

    load_k.wait()
    direct(0)
    tell(0)

    def group(s):
        gg = lax.rem(g + s, ng)
        xx = lax.div(gg, 2)
        kk = lax.rem(gg, 2)
        return gg, xx, kk, {"dp": y * nx + xx, "ctx": 2 * z + kk}

    def columns_to(s):
        gg, xx, kk, device = group(s)
        return remote(x_out.at[gg], xg.at[g], xg_send, xg_recv, device)

    def all_columns():
        return remote(x_out.at[pl.ds(0, ng - 1)], xg.at[pl.ds(0, ng - 1)], xg_send, xg_recv, sibling)

    load_x.wait()
    load_w.wait()
    v_all[c] = dot(x_v[...], w_v[...]).astype(jnp.bfloat16)
    for gg in range(ng):
        for i in range(yc):
            column = (((gg % 2) * yc + i) * nx + gg // 2) * BLOCK
            x_out[gg, i] = x_v[:, column : column + BLOCK]
    load_q.wait()
    load_gc.wait()
    for h in range(heads):
        part = q_v[:, h * BLOCK : (h + 1) * BLOCK]
        rows = slice((h % 2) * BLOCK, (h % 2 + 1) * BLOCK)
        qn[h // 2, rows, :] = part
        qt[h // 2, :, rows] = part.T
        gcn[h // 2, rows, :] = gc_v[:, h * BLOCK : (h + 1) * BLOCK]

    relay(0)
    direct(1)
    hear(0)
    tell(1)

    block = ord_s[0, c]
    first = jnp.maximum(block - (wb - 1), 0)
    query_pos = block * BLOCK + lax.broadcasted_iota(jnp.int32, (1, BLOCK), 1)
    low = jnp.zeros((1, BLOCK), jnp.int32)
    end = jnp.int32(0)
    for i in range(len_s.shape[1]):
        end = end + len_s[0, i]
        low = jnp.where(query_pos >= end, end, low)
    key_pos = first * BLOCK + lax.broadcasted_iota(jnp.int32, (span, BLOCK), 0)
    bias[...] = jnp.where((key_pos >= low) & (key_pos <= query_pos), 0.0, NEG)
    kacc[...] = jnp.zeros_like(kacc)
    vacc[...] = jnp.zeros_like(vacc)
    for t in range(2):
        for i in range(pb + nc):
            if i < pb or i >= pb + wb:
                pad[t, i] = jnp.zeros((BLOCK, BLOCK), jnp.bfloat16)
    for h in range(heads):
        rows = slice((h % 2) * BLOCK, (h % 2 + 1) * BLOCK)
        gct[h // 2, :, rows] = gc_v[:, h * BLOCK : (h + 1) * BLOCK].T

    settle(0)
    hear(1)
    tell(2)
    for s in range(1, ng):
        columns_to(s).start()
    all_siblings(0).wait_recv()

    for i in range(wb):
        kw[i * BLOCK : (i + 1) * BLOCK, :] = k_all[first + i]
    log_scale = score_scale * math.log2(math.e)

    def weigh(p, carry):
        scores = dot(kw[...], qt[p]) + jnp.concatenate([bias[...], bias[...]], axis=1)
        row_max = jnp.max(scores, axis=0, keepdims=True)
        exp_scores = jnp.exp2(scores * log_scale - row_max * log_scale)
        weights = (exp_scores * (1.0 / jnp.sum(exp_scores, axis=0, keepdims=True))).astype(
            jnp.bfloat16
        )
        wt[p] = weights
        vacc[...] += dot(weights, gcn[p])
        return carry

    lax.fori_loop(0, pairs // 2, weigh, 0, unroll=True)
    relay(1)
    lax.fori_loop(pairs // 2, pairs, weigh, 0, unroll=True)

    def half(t):
        return remote(sib_out.at[t], sib_in.at[t], half_send.at[t], half_recv.at[t], sibling)

    def swap_halves(t, acc, factor):
        for i in range(wb):
            pad[t, pb + i] = (acc[i * BLOCK : (i + 1) * BLOCK, :] * factor).astype(jnp.bfloat16)
        for zs in range(nz):
            sib_out[t, zs] = pad[t, pb + 2 * zs + 1 - k - first]
        half(t).start()

    parts = {0: (slice(0, BLOCK),), 1: (slice(0, BLOCK // 2), slice(BLOCK // 2, BLOCK))}

    def scatter(t, s, n):
        rows = parts[t][n]
        return remote(
            rs_out.at[t, at(s), rows], rs_in.at[t, z, rows], rs_send.at[t + n], rs_recv.at[t + n],
            {"ctx": 2 * at(s) + k},
        )

    def all_scattered(t, n):
        many = pl.ds(0, nz - 1)
        return remote(
            rs_out.at[t, many, parts[t][n]], rs_in.at[t, many, parts[t][n]],
            rs_send.at[t + n], rs_recv.at[t + n], sibling,
        )

    def scatter_sums(t):
        half(t).wait_recv()
        for zs in range(nz):
            both = pad[t, pb + 2 * zs + k - first].astype(jnp.float32) + sib_in[t, zs].astype(
                jnp.float32
            )
            rs_out[t, zs] = both.astype(jnp.bfloat16)
        for n in range(len(parts[t])):
            for s in sorted(range(1, nz), key=lambda s: -min(s, nz - s)):
                scatter(t, s, n).start()

    def gathered(t, n):
        all_scattered(t, n).wait_recv()
        total = rs_out[t, z, parts[t][n]].astype(jnp.float32)
        for s in range(1, nz):
            total += rs_in[t, at(s), parts[t][n]].astype(jnp.float32)
        return total.astype(jnp.bfloat16)

    swap_halves(1, vacc, 1.0)
    scatter_sums(1)
    settle(1)
    hear(2)
    tell(3)

    for i in range(wb):
        kwt[:, i * BLOCK : (i + 1) * BLOCK] = kw[i * BLOCK : (i + 1) * BLOCK, :].T
    all_siblings(1).wait_recv()
    for i in range(wb):
        value_block = v_all[first + i]
        vw[i * BLOCK : (i + 1) * BLOCK, :] = value_block
        vwt[:, i * BLOCK : (i + 1) * BLOCK] = value_block.T

    def attend(p, carry):
        weights = wt[p]
        turned = gct[p]
        context = dot(vwt[...], weights).astype(jnp.bfloat16)
        delta = jnp.sum(
            turned.astype(jnp.float32) * context.astype(jnp.float32), axis=0, keepdims=True
        )
        grad_prob = dot(vw[...], turned)
        grad_scores = (weights.astype(jnp.float32) * (grad_prob - delta)).astype(jnp.bfloat16)
        grad_query = (dot(kwt[...], grad_scores) * score_scale).astype(jnp.bfloat16)
        kacc[...] += dot(grad_scores, qn[p])
        for i in range(2):
            columns = pl.ds(pl.multiple_of((2 * p + i) * BLOCK, BLOCK), BLOCK)
            lanes = slice(i * BLOCK, (i + 1) * BLOCK)
            ctx_v[:, columns] = context[:, lanes].T
            gq_v[:, columns] = grad_query[:, lanes].T
        return carry

    lax.fori_loop(0, pairs, attend, 0, unroll=True)
    store_ctx = pltpu.make_async_copy(ctx_v, ctx_o, store_sem.at[0])
    store_gq = pltpu.make_async_copy(gq_v, gq_o, store_sem.at[1])
    swap_halves(0, kacc, score_scale)
    store_ctx.start()
    store_gq.start()

    def share(s, n):
        gg, xx, kk, device = group(s)
        rows = gvg.at[g, parts[1][n]]
        return remote(rows, rows, gv_send.at[n], gv_recv.at[n], device)

    def all_shared(n):
        rows = gvg.at[pl.ds(0, ng - 1), parts[1][n]]
        return remote(rows, rows, gv_send.at[n], gv_recv.at[n], sibling)

    for n in range(2):
        gvg[g, parts[1][n]] = gathered(1, n)
        for s in sorted(range(1, ng), key=lambda s: -min(s, ng - s)):
            share(s, n).start()
    scatter_sums(0)

    all_columns().wait_recv()
    xg[g] = x_out[g]
    for gg in range(ng):
        for i in range(yc):
            xgt[i, :, gg * BLOCK : (gg + 1) * BLOCK] = xg[gg, i].T
    hear(3)

    store_gv = pltpu.make_async_copy(gvg.at[g], gv_o, store_sem.at[2])
    store_gv.start()
    all_shared(0).wait_recv()
    all_shared(1).wait_recv()

    group_rows = gvg[...].reshape(ng * BLOCK, BLOCK)
    source_core = lax.div(y, yc)

    def to_y(i, kk):
        yy = k * yc + i
        return (yy != y) | (kk != k), remote(
            p_out.at[2 * i + kk], p_in.at[y], p_send, p_recv,
            {"dp": yy * nx + x, "ctx": 2 * z + kk},
        )

    def all_y(count):
        return remote(p_out.at[pl.ds(0, count)], p_in.at[pl.ds(0, count)], p_send, p_recv, sibling)

    for i in range(yc):
        product = dot(xgt[i], group_rows).reshape(nz, 2, fr, BLOCK)
        for kk in range(2):
            p_out[2 * i + kk] = product[:, kk].reshape(nz * fr, BLOCK).astype(jnp.bfloat16)
            away, copy = to_y(i, kk)
            pl.when(away)(copy.start)

    @pl.when(source_core == k)
    def _():
        all_y(ny - 1).wait_recv()
        p_in[y] = p_out[2 * lax.rem(y, yc) + k]

    @pl.when(source_core != k)
    def _():
        all_y(ny).wait_recv()

    r_v[...] = jnp.sum(p_in[...].astype(jnp.float32), axis=0)

    def to_z(zs):
        rows = pl.ds(zs * fr, fr)
        return remote(
            r_v.at[rows], r_in.at[z], r_send, r_recv, {"ctx": 2 * zs + k}
        )

    for zs in range(nz):
        pl.when(zs != z)(to_z(zs).start)

    gkv_v[...] = gathered(0, 0)
    store_gk = pltpu.make_async_copy(gkv_v, gk_o, store_sem.at[3])
    store_gk.start()

    def all_z():
        return remote(
            r_in.at[pl.ds(0, nz - 1)], r_in.at[pl.ds(0, nz - 1)], r_send, r_recv, sibling
        )

    all_z().wait_recv()
    total = r_v[pl.ds(pl.multiple_of(z * fr, fr), fr), :]
    for s in range(1, nz):
        total += r_in[at(s)]
    gw_v[...] = total
    store_gw = pltpu.make_async_copy(gw_v, gw_o, store_sem.at[4])
    store_gw.start()

    for t in range(2):
        hops(t, 0, nz - 1).wait_send()
        all_siblings(t).wait_send()
        half(t).wait_send()
        for n in range(len(parts[t])):
            all_scattered(t, n).wait_send()
    all_columns().wait_send()
    all_shared(0).wait_send()
    all_shared(1).wait_send()
    pl.when(source_core == k)(all_y(2 * yc - 1).wait_send)
    pl.when(source_core != k)(all_y(2 * yc).wait_send)
    all_z().wait_send()

    for one in (store_ctx, store_gq, store_gv, store_gk, store_gw):
        one.wait()


def write_out(*refs):
    held, sems = refs[10:15], refs[15]
    for i in range(5):
        pltpu.make_async_copy(refs[i], held[i], sems.at[0, i]).start()
    for i in range(5):
        pltpu.make_async_copy(refs[i], held[i], sems.at[0, i]).wait()
        pltpu.make_async_copy(held[i], refs[5 + i], sems.at[1, i]).start()
    for i in range(5):
        pltpu.make_async_copy(held[i], refs[5 + i], sems.at[1, i]).wait()


def body(nx, ny, nz, queries, key_rows, x_rows, value_weight, grad_context, doc_lengths, block_order):
    rows, width = queries.shape[1:]
    features = x_rows.shape[2]
    heads = width // BLOCK
    nc = 2 * nz
    wb = nc // 2 + 1
    pb = nc - wb
    yc = ny // 2
    ng = 2 * nx
    fr = BLOCK // nc
    pairs = heads // 2
    span = wb * BLOCK
    bf16, f32 = jnp.bfloat16, jnp.float32
    sq = (BLOCK, BLOCK)
    anywhere = pl.BlockSpec(memory_space=pltpu.HBM)
    scalars = pl.BlockSpec(memory_space=pltpu.SMEM)
    dma = pltpu.SemaphoreType.DMA
    outs = pl.pallas_call(
        functools.partial(kernel, nx, ny, nz, heads),
        out_shape=(
            jax.ShapeDtypeStruct((rows, width), bf16),
            jax.ShapeDtypeStruct((rows, width), bf16),
            jax.ShapeDtypeStruct(sq, bf16),
            jax.ShapeDtypeStruct(sq, bf16),
            jax.ShapeDtypeStruct((fr, BLOCK), f32),
        ),
        in_specs=[anywhere] * 5 + [scalars] * 2,
        out_specs=(anywhere,) * 5,
        scratch_shapes=[
            pltpu.VMEM((rows, width), bf16),
            pltpu.VMEM((rows, width), bf16),
            pltpu.VMEM((rows, features), bf16),
            pltpu.VMEM((features, BLOCK), bf16),
            pltpu.VMEM((nc,) + sq, bf16),
            pltpu.VMEM((nc,) + sq, bf16),
            pltpu.VMEM((pairs, 2 * BLOCK, BLOCK), bf16),
            pltpu.VMEM((pairs, BLOCK, 2 * BLOCK), bf16),
            pltpu.VMEM((pairs, 2 * BLOCK, BLOCK), bf16),
            pltpu.VMEM((pairs, BLOCK, 2 * BLOCK), bf16),
            pltpu.VMEM((span, BLOCK), f32),
            pltpu.VMEM((span, BLOCK), bf16),
            pltpu.VMEM((span, BLOCK), bf16),
            pltpu.VMEM((BLOCK, span), bf16),
            pltpu.VMEM((BLOCK, span), bf16),
            pltpu.VMEM((pairs, span, 2 * BLOCK), bf16),
            pltpu.VMEM((span, BLOCK), f32),
            pltpu.VMEM((span, BLOCK), f32),
            pltpu.VMEM((2, pb + nc) + sq, bf16),
            pltpu.VMEM((2, nz) + sq, bf16),
            pltpu.VMEM((2, nz) + sq, bf16),
            pltpu.VMEM((2, nz) + sq, bf16),
            pltpu.VMEM((2, nz) + sq, bf16),
            pltpu.VMEM((rows, width), bf16),
            pltpu.VMEM((rows, width), bf16),
            pltpu.VMEM(sq, bf16),
            pltpu.VMEM((ng, yc) + sq, bf16),
            pltpu.VMEM((ng, yc) + sq, bf16),
            pltpu.VMEM((yc, BLOCK, ng * BLOCK), bf16),
            pltpu.VMEM((ng,) + sq, bf16),
            pltpu.VMEM((2 * yc, nz * fr, BLOCK), bf16),
            pltpu.VMEM((ny, nz * fr, BLOCK), bf16),
            pltpu.VMEM((nz * fr, BLOCK), f32),
            pltpu.VMEM((nz, fr, BLOCK), f32),
            pltpu.VMEM((fr, BLOCK), f32),
            pltpu.SemaphoreType.REGULAR((4,)),
            dma((5,)),
            dma((5,)),
            dma((2,)),
            dma((2, 4)),
            dma((2,)),
            dma((2,)),
            dma((2,)),
            dma((2,)),
            dma((3,)),
            dma((3,)),
            dma,
            dma,
            dma((2,)),
            dma((2,)),
            dma,
            dma,
            dma,
            dma,
        ],
        compiler_params=pltpu.CompilerParams(
            collective_id=0, has_side_effects=True, vmem_limit_bytes=VMEM_LIMIT
        ),
        name="attention_core",
    )(
        queries[0], key_rows[0], x_rows[0], value_weight, grad_context[0], doc_lengths, block_order
    )
    context, grad_queries, grad_keys, grad_values, grad_weight = pl.pallas_call(
        write_out,
        out_shape=tuple(jax.ShapeDtypeStruct(one.shape, one.dtype) for one in outs),
        in_specs=[anywhere] * 5,
        out_specs=(anywhere,) * 5,
        scratch_shapes=[pltpu.VMEM(one.shape, one.dtype) for one in outs] + [dma((2, 5))],
        compiler_params=pltpu.CompilerParams(vmem_limit_bytes=VMEM_LIMIT),
        name="write_out",
    )(*outs)
    return (context[None], grad_queries[None], grad_keys[None], grad_values[None], grad_weight)


def solution(mesh, sizes=(4, 8, 8)):
    placed = (
        P("dp", "ctx", None),
        P("dp", "ctx", None),
        P("dp", "ctx", None),
        P(),
        P("dp", "ctx", None),
        P("dp", None),
        P("dp", None),
    )
    return jax.shard_map(
        functools.partial(body, *sizes),
        mesh=mesh,
        in_specs=placed,
        out_specs=(
            P("dp", "ctx", None),
            P("dp", "ctx", None),
            P("dp", "ctx", None),
            P("dp", "ctx", None),
            P(("dp", "ctx"), None),
        ),
        check_vma=False,
    )
```

```python
import functools
import math

import jax
import jax.numpy as jnp
from jax import lax
from jax.experimental import pallas as pl
from jax.experimental.pallas import tpu as pltpu
from jax.sharding import PartitionSpec as P

BLOCK = 128
MESH = pl.DeviceIdType.MESH
NEG = -1e30
VMEM_LIMIT = 60 * 1024 * 1024


def remote(src, dst, send_sem, recv_sem, device):
    return pltpu.make_async_remote_copy(
        src_ref=src,
        dst_ref=dst,
        send_sem=send_sem,
        recv_sem=recv_sem,
        device_id=device,
        device_id_type=MESH,
    )


def dot(a, b):
    return jnp.dot(a, b, preferred_element_type=jnp.float32)


def kernel(
    nx, ny, nz, heads,
    q_hbm, k_hbm, x_hbm, w_hbm, gc_hbm, len_s, ord_s,
    ctx_o, gq_o, gk_o, gv_o, gw_o,
    q_v, gc_v, x_v, w_v, k_all, v_all, qn, qt, gcn, gct, bias, kw, vw, kwt, vwt,
    wt, kacc, vacc, pad, sib_out, sib_in, rs_out, rs_in, ctx_v, gq_v, gkv_v,
    x_out, xg, xgt, gvg, p_out, p_in, r_v, r_in, gw_v,
    ready, load_sem, store_sem, hop_send, hop_recv, sib_send, sib_recv,
    half_send, half_recv, rs_send, rs_recv, xg_send, xg_recv,
    gv_send, gv_recv, p_send, p_recv, r_send, r_recv,
):
    nc = 2 * nz
    wb = nc // 2 + 1
    pb = nc - wb
    yc = ny // 2
    ng = 2 * nx
    fr = BLOCK // nc
    pairs = heads // 2
    span = wb * BLOCK
    d = lax.axis_index("dp")
    c = lax.axis_index("ctx")
    y = lax.div(d, nx)
    x = lax.rem(d, nx)
    z = lax.div(c, 2)
    k = lax.rem(c, 2)
    g = 2 * x + k
    kv = (k_all, v_all)
    score_scale = 1.0 / math.sqrt(BLOCK)

    sibling = {"ctx": 2 * z + 1 - k}

    def load(src, dst, n):
        return pltpu.make_async_copy(src, dst, load_sem.at[n])

    load_k = load(k_hbm, k_all.at[c], 0)
    load_x = load(x_hbm, x_v, 1)
    load_w = load(w_hbm, w_v, 2)
    load_q = load(q_hbm, q_v, 3)
    load_gc = load(gc_hbm, gc_v, 4)
    load_k.start()

    barrier = pltpu.get_barrier_semaphore()

    def around(n, most):
        return sorted({s % n for s in range(-most, most + 1)} - {0})

    planar = [{"dp": y * nx + lax.rem(x + s, nx)} for s in around(nx, 1)]
    planar += [{"dp": lax.rem(y + s, ny) * nx + x} for s in around(ny, 1)]
    planar.append(sibling)
    partners = planar + [{"ctx": 2 * lax.rem(z + s, nz) + k} for s in around(nz, 2)]
    for device in partners:
        pl.semaphore_signal(barrier, 1, device_id=device, device_id_type=MESH)
    for one in (load_q, load_x, load_w, load_gc):
        one.start()
    pl.semaphore_wait(barrier, len(partners))

    def tell(n):
        for device in planar:
            pl.semaphore_signal(ready.at[n], 1, device_id=device, device_id_type=MESH)

    def hear(n):
        pl.semaphore_wait(ready.at[n], len(planar))


    def at(s):
        return lax.rem(z + (s + 2 * nz), nz)

    def hop(t, zs, s, kind, part=None):
        slot = kv[t].at[2 * zs + k]
        if part is not None:
            slot = slot.at[pl.ds(part * (BLOCK // 2), BLOCK // 2)]
        return remote(slot, slot, hop_send.at[t], hop_recv.at[t, kind], {"ctx": 2 * at(s) + k})

    def hops(t, kind, count):
        slots = kv[t].at[pl.ds(0, count)]
        return remote(slots, slots, hop_send.at[t], hop_recv.at[t, kind], sibling)

    def to_sibling(t, zs):
        slot = kv[t].at[2 * zs + k]
        return remote(slot, slot, sib_send.at[t], sib_recv.at[t], sibling)

    def all_siblings(t):
        slots = kv[t].at[pl.ds(0, nz)]
        return remote(slots, slots, sib_send.at[t], sib_recv.at[t], sibling)

    relayed = nz == 8
    close = (1, -1) if nz > 2 else (1,)
    if nz == 4:
        close = (2, 1, -1)

    def direct(t):
        if relayed:
            hop(t, z, 2, 0).start()
            hop(t, z, -2, 1).start()
        for s in close:
            hop(t, z, s, 2).start()
        to_sibling(t, z).start()

    def relay(t):
        if relayed:
            for kind, s in ((0, 1), (1, -1)):
                zs = at(-2 * s)
                hops(t, kind, 1).wait_recv()
                hop(t, zs, 2 * s, 3, kind).start()
                hop(t, zs, s, 3).start()
                to_sibling(t, zs).start()
        hops(t, 2, len(close)).wait_recv()
        for s in close:
            to_sibling(t, at(-s)).start()

    def settle(t):
        if relayed:
            hops(t, 3, 3).wait_recv()
            for s in (3, -3, 4):
                to_sibling(t, at(s)).start()

    load_k.wait()
    direct(0)
    tell(0)

    def group(s):
        gg = lax.rem(g + s, ng)
        xx = lax.div(gg, 2)
        kk = lax.rem(gg, 2)
        return gg, xx, kk, {"dp": y * nx + xx, "ctx": 2 * z + kk}

    def columns_to(s):
        gg, xx, kk, device = group(s)
        return remote(x_out.at[gg], xg.at[g], xg_send, xg_recv, device)

    def all_columns():
        return remote(x_out.at[pl.ds(0, ng - 1)], xg.at[pl.ds(0, ng - 1)], xg_send, xg_recv, sibling)

    load_x.wait()
    load_w.wait()
    v_all[c] = dot(x_v[...], w_v[...]).astype(jnp.bfloat16)
    for gg in range(ng):
        for i in range(yc):
            column = (((gg % 2) * yc + i) * nx + gg // 2) * BLOCK
            x_out[gg, i] = x_v[:, column : column + BLOCK]
    load_q.wait()
    load_gc.wait()
    for h in range(heads):
        part = q_v[:, h * BLOCK : (h + 1) * BLOCK]
        rows = slice((h % 2) * BLOCK, (h % 2 + 1) * BLOCK)
        qn[h // 2, rows, :] = part
        qt[h // 2, :, rows] = part.T
        gcn[h // 2, rows, :] = gc_v[:, h * BLOCK : (h + 1) * BLOCK]

    relay(0)
    direct(1)
    hear(0)
    tell(1)

    block = ord_s[0, c]
    first = jnp.maximum(block - (wb - 1), 0)
    query_pos = block * BLOCK + lax.broadcasted_iota(jnp.int32, (1, BLOCK), 1)
    low = jnp.zeros((1, BLOCK), jnp.int32)
    end = jnp.int32(0)
    for i in range(len_s.shape[1]):
        end = end + len_s[0, i]
        low = jnp.where(query_pos >= end, end, low)
    key_pos = first * BLOCK + lax.broadcasted_iota(jnp.int32, (span, BLOCK), 0)
    bias[...] = jnp.where((key_pos >= low) & (key_pos <= query_pos), 0.0, NEG)
    kacc[...] = jnp.zeros_like(kacc)
    vacc[...] = jnp.zeros_like(vacc)
    for t in range(2):
        for i in range(pb + nc):
            if i < pb or i >= pb + wb:
                pad[t, i] = jnp.zeros((BLOCK, BLOCK), jnp.bfloat16)
    for h in range(heads):
        rows = slice((h % 2) * BLOCK, (h % 2 + 1) * BLOCK)
        gct[h // 2, :, rows] = gc_v[:, h * BLOCK : (h + 1) * BLOCK].T

    settle(0)
    hear(1)
    tell(2)
    for s in range(1, ng):
        columns_to(s).start()
    all_siblings(0).wait_recv()

    for i in range(wb):
        kw[i * BLOCK : (i + 1) * BLOCK, :] = k_all[first + i]
    log_scale = score_scale * math.log2(math.e)

    def weigh(p):
        scores = dot(kw[...], qt[p]) + jnp.concatenate([bias[...], bias[...]], axis=1)
        row_max = jnp.max(scores, axis=0, keepdims=True)
        exp_scores = jnp.exp2(scores * log_scale - row_max * log_scale)
        wt[:, 2 * BLOCK * p : 2 * BLOCK * (p + 1)] = (
            exp_scores * (1.0 / jnp.sum(exp_scores, axis=0, keepdims=True))
        ).astype(jnp.bfloat16)

    for p in range(pairs // 2):
        weigh(p)
    relay(1)
    for p in range(pairs // 2, pairs):
        weigh(p)
    vacc[...] = dot(wt[...], gcn[...].reshape(heads * BLOCK, BLOCK))

    def half(t):
        return remote(sib_out.at[t], sib_in.at[t], half_send.at[t], half_recv.at[t], sibling)

    def swap_halves(t, acc, factor):
        for i in range(wb):
            pad[t, pb + i] = (acc[i * BLOCK : (i + 1) * BLOCK, :] * factor).astype(jnp.bfloat16)
        for zs in range(nz):
            sib_out[t, zs] = pad[t, pb + 2 * zs + 1 - k - first]
        half(t).start()

    parts = {0: (slice(0, BLOCK),), 1: (slice(0, BLOCK // 2), slice(BLOCK // 2, BLOCK))}

    def scatter(t, s, n):
        rows = parts[t][n]
        return remote(
            rs_out.at[t, at(s), rows], rs_in.at[t, z, rows], rs_send.at[t + n], rs_recv.at[t + n],
            {"ctx": 2 * at(s) + k},
        )

    def all_scattered(t, n):
        many = pl.ds(0, nz - 1)
        return remote(
            rs_out.at[t, many, parts[t][n]], rs_in.at[t, many, parts[t][n]],
            rs_send.at[t + n], rs_recv.at[t + n], sibling,
        )

    def scatter_sums(t):
        half(t).wait_recv()
        for zs in range(nz):
            both = pad[t, pb + 2 * zs + k - first].astype(jnp.float32) + sib_in[t, zs].astype(
                jnp.float32
            )
            rs_out[t, zs] = both.astype(jnp.bfloat16)
        for n in range(len(parts[t])):
            for s in sorted(range(1, nz), key=lambda s: -min(s, nz - s)):
                scatter(t, s, n).start()

    def gathered(t, n):
        all_scattered(t, n).wait_recv()
        total = rs_out[t, z, parts[t][n]].astype(jnp.float32)
        for s in range(1, nz):
            total += rs_in[t, at(s), parts[t][n]].astype(jnp.float32)
        return total.astype(jnp.bfloat16)

    swap_halves(1, vacc, 1.0)
    scatter_sums(1)
    settle(1)
    hear(2)
    tell(3)

    for i in range(wb):
        kwt[:, i * BLOCK : (i + 1) * BLOCK] = kw[i * BLOCK : (i + 1) * BLOCK, :].T
    all_siblings(1).wait_recv()
    for i in range(wb):
        value_block = v_all[first + i]
        vw[i * BLOCK : (i + 1) * BLOCK, :] = value_block
        vwt[:, i * BLOCK : (i + 1) * BLOCK] = value_block.T

    def attend(p, carry):
        weights = wt[:, pl.ds(pl.multiple_of(p * 2 * BLOCK, 2 * BLOCK), 2 * BLOCK)]
        turned = gct[p]
        context = dot(vwt[...], weights).astype(jnp.bfloat16)
        delta = jnp.sum(
            turned.astype(jnp.float32) * context.astype(jnp.float32), axis=0, keepdims=True
        )
        grad_prob = dot(vw[...], turned)
        grad_scores = (weights.astype(jnp.float32) * (grad_prob - delta)).astype(jnp.bfloat16)
        grad_query = (dot(kwt[...], grad_scores) * score_scale).astype(jnp.bfloat16)
        kacc[...] += dot(grad_scores, qn[p])
        for i in range(2):
            columns = pl.ds(pl.multiple_of((2 * p + i) * BLOCK, BLOCK), BLOCK)
            lanes = slice(i * BLOCK, (i + 1) * BLOCK)
            ctx_v[:, columns] = context[:, lanes].T
            gq_v[:, columns] = grad_query[:, lanes].T
        return carry

    lax.fori_loop(0, pairs, attend, 0, unroll=True)
    store_ctx = pltpu.make_async_copy(ctx_v, ctx_o, store_sem.at[0])
    store_gq = pltpu.make_async_copy(gq_v, gq_o, store_sem.at[1])
    swap_halves(0, kacc, score_scale)
    store_ctx.start()
    store_gq.start()

    def share(s, n):
        gg, xx, kk, device = group(s)
        rows = gvg.at[g, parts[1][n]]
        return remote(rows, rows, gv_send.at[n], gv_recv.at[n], device)

    def all_shared(n):
        rows = gvg.at[pl.ds(0, ng - 1), parts[1][n]]
        return remote(rows, rows, gv_send.at[n], gv_recv.at[n], sibling)

    for n in range(2):
        gvg[g, parts[1][n]] = gathered(1, n)
        for s in sorted(range(1, ng), key=lambda s: -min(s, ng - s)):
            share(s, n).start()
    scatter_sums(0)

    all_columns().wait_recv()
    xg[g] = x_out[g]
    for gg in range(ng):
        for i in range(yc):
            xgt[i, :, gg * BLOCK : (gg + 1) * BLOCK] = xg[gg, i].T
    hear(3)

    store_gv = pltpu.make_async_copy(gvg.at[g], gv_o, store_sem.at[2])
    store_gv.start()
    all_shared(0).wait_recv()
    all_shared(1).wait_recv()

    group_rows = gvg[...].reshape(ng * BLOCK, BLOCK)
    source_core = lax.div(y, yc)

    def to_y(i, kk):
        yy = k * yc + i
        return (yy != y) | (kk != k), remote(
            p_out.at[2 * i + kk], p_in.at[y], p_send, p_recv,
            {"dp": yy * nx + x, "ctx": 2 * z + kk},
        )

    def all_y(count):
        return remote(p_out.at[pl.ds(0, count)], p_in.at[pl.ds(0, count)], p_send, p_recv, sibling)

    for i in range(yc):
        product = dot(xgt[i], group_rows).reshape(nz, 2, fr, BLOCK)
        for kk in range(2):
            p_out[2 * i + kk] = product[:, kk].reshape(nz * fr, BLOCK).astype(jnp.bfloat16)
            away, copy = to_y(i, kk)
            pl.when(away)(copy.start)

    @pl.when(source_core == k)
    def _():
        all_y(ny - 1).wait_recv()
        p_in[y] = p_out[2 * lax.rem(y, yc) + k]

    @pl.when(source_core != k)
    def _():
        all_y(ny).wait_recv()

    r_v[...] = jnp.sum(p_in[...].astype(jnp.float32), axis=0)

    def to_z(zs):
        rows = pl.ds(zs * fr, fr)
        return remote(
            r_v.at[rows], r_in.at[z], r_send, r_recv, {"ctx": 2 * zs + k}
        )

    for zs in range(nz):
        pl.when(zs != z)(to_z(zs).start)

    gkv_v[...] = gathered(0, 0)
    store_gk = pltpu.make_async_copy(gkv_v, gk_o, store_sem.at[3])
    store_gk.start()

    def all_z():
        return remote(
            r_in.at[pl.ds(0, nz - 1)], r_in.at[pl.ds(0, nz - 1)], r_send, r_recv, sibling
        )

    all_z().wait_recv()
    total = r_v[pl.ds(pl.multiple_of(z * fr, fr), fr), :]
    for s in range(1, nz):
        total += r_in[at(s)]
    gw_v[...] = total
    store_gw = pltpu.make_async_copy(gw_v, gw_o, store_sem.at[4])
    store_gw.start()

    for t in range(2):
        hops(t, 0, nz - 1).wait_send()
        all_siblings(t).wait_send()
        half(t).wait_send()
        for n in range(len(parts[t])):
            all_scattered(t, n).wait_send()
    all_columns().wait_send()
    all_shared(0).wait_send()
    all_shared(1).wait_send()
    pl.when(source_core == k)(all_y(2 * yc - 1).wait_send)
    pl.when(source_core != k)(all_y(2 * yc).wait_send)
    all_z().wait_send()

    for one in (store_ctx, store_gq, store_gv, store_gk, store_gw):
        one.wait()


def write_out(*refs):
    held, sems = refs[10:15], refs[15]
    for i in range(5):
        pltpu.make_async_copy(refs[i], held[i], sems.at[0, i]).start()
    for i in range(5):
        pltpu.make_async_copy(refs[i], held[i], sems.at[0, i]).wait()
        pltpu.make_async_copy(held[i], refs[5 + i], sems.at[1, i]).start()
    for i in range(5):
        pltpu.make_async_copy(held[i], refs[5 + i], sems.at[1, i]).wait()


def body(nx, ny, nz, queries, key_rows, x_rows, value_weight, grad_context, doc_lengths, block_order):
    rows, width = queries.shape[1:]
    features = x_rows.shape[2]
    heads = width // BLOCK
    nc = 2 * nz
    wb = nc // 2 + 1
    pb = nc - wb
    yc = ny // 2
    ng = 2 * nx
    fr = BLOCK // nc
    pairs = heads // 2
    span = wb * BLOCK
    bf16, f32 = jnp.bfloat16, jnp.float32
    sq = (BLOCK, BLOCK)
    anywhere = pl.BlockSpec(memory_space=pltpu.HBM)
    scalars = pl.BlockSpec(memory_space=pltpu.SMEM)
    dma = pltpu.SemaphoreType.DMA
    outs = pl.pallas_call(
        functools.partial(kernel, nx, ny, nz, heads),
        out_shape=(
            jax.ShapeDtypeStruct((rows, width), bf16),
            jax.ShapeDtypeStruct((rows, width), bf16),
            jax.ShapeDtypeStruct(sq, bf16),
            jax.ShapeDtypeStruct(sq, bf16),
            jax.ShapeDtypeStruct((fr, BLOCK), f32),
        ),
        in_specs=[anywhere] * 5 + [scalars] * 2,
        out_specs=(anywhere,) * 5,
        scratch_shapes=[
            pltpu.VMEM((rows, width), bf16),
            pltpu.VMEM((rows, width), bf16),
            pltpu.VMEM((rows, features), bf16),
            pltpu.VMEM((features, BLOCK), bf16),
            pltpu.VMEM((nc,) + sq, bf16),
            pltpu.VMEM((nc,) + sq, bf16),
            pltpu.VMEM((pairs, 2 * BLOCK, BLOCK), bf16),
            pltpu.VMEM((pairs, BLOCK, 2 * BLOCK), bf16),
            pltpu.VMEM((pairs, 2 * BLOCK, BLOCK), bf16),
            pltpu.VMEM((pairs, BLOCK, 2 * BLOCK), bf16),
            pltpu.VMEM((span, BLOCK), f32),
            pltpu.VMEM((span, BLOCK), bf16),
            pltpu.VMEM((span, BLOCK), bf16),
            pltpu.VMEM((BLOCK, span), bf16),
            pltpu.VMEM((BLOCK, span), bf16),
            pltpu.VMEM((span, heads * BLOCK), bf16),
            pltpu.VMEM((span, BLOCK), f32),
            pltpu.VMEM((span, BLOCK), f32),
            pltpu.VMEM((2, pb + nc) + sq, bf16),
            pltpu.VMEM((2, nz) + sq, bf16),
            pltpu.VMEM((2, nz) + sq, bf16),
            pltpu.VMEM((2, nz) + sq, bf16),
            pltpu.VMEM((2, nz) + sq, bf16),
            pltpu.VMEM((rows, width), bf16),
            pltpu.VMEM((rows, width), bf16),
            pltpu.VMEM(sq, bf16),
            pltpu.VMEM((ng, yc) + sq, bf16),
            pltpu.VMEM((ng, yc) + sq, bf16),
            pltpu.VMEM((yc, BLOCK, ng * BLOCK), bf16),
            pltpu.VMEM((ng,) + sq, bf16),
            pltpu.VMEM((2 * yc, nz * fr, BLOCK), bf16),
            pltpu.VMEM((ny, nz * fr, BLOCK), bf16),
            pltpu.VMEM((nz * fr, BLOCK), f32),
            pltpu.VMEM((nz, fr, BLOCK), f32),
            pltpu.VMEM((fr, BLOCK), f32),
            pltpu.SemaphoreType.REGULAR((4,)),
            dma((5,)),
            dma((5,)),
            dma((2,)),
            dma((2, 4)),
            dma((2,)),
            dma((2,)),
            dma((2,)),
            dma((2,)),
            dma((3,)),
            dma((3,)),
            dma,
            dma,
            dma((2,)),
            dma((2,)),
            dma,
            dma,
            dma,
            dma,
        ],
        compiler_params=pltpu.CompilerParams(
            collective_id=0, has_side_effects=True, vmem_limit_bytes=VMEM_LIMIT
        ),
        name="attention_core",
    )(
        queries[0], key_rows[0], x_rows[0], value_weight, grad_context[0], doc_lengths, block_order
    )
    context, grad_queries, grad_keys, grad_values, grad_weight = pl.pallas_call(
        write_out,
        out_shape=tuple(jax.ShapeDtypeStruct(one.shape, one.dtype) for one in outs),
        in_specs=[anywhere] * 5,
        out_specs=(anywhere,) * 5,
        scratch_shapes=[pltpu.VMEM(one.shape, one.dtype) for one in outs] + [dma((2, 5))],
        compiler_params=pltpu.CompilerParams(vmem_limit_bytes=VMEM_LIMIT),
        name="write_out",
    )(*outs)
    return (context[None], grad_queries[None], grad_keys[None], grad_values[None], grad_weight)


def solution(mesh, sizes=(4, 8, 8)):
    placed = (
        P("dp", "ctx", None),
        P("dp", "ctx", None),
        P("dp", "ctx", None),
        P(),
        P("dp", "ctx", None),
        P("dp", None),
        P("dp", None),
    )
    return jax.shard_map(
        functools.partial(body, *sizes),
        mesh=mesh,
        in_specs=placed,
        out_specs=(
            P("dp", "ctx", None),
            P("dp", "ctx", None),
            P("dp", "ctx", None),
            P("dp", "ctx", None),
            P(("dp", "ctx"), None),
        ),
        check_vma=False,
    )
```
